32 devices in a mesh: group: 2 (over x), tm: 4 (over y, core), tensor: 4 (over z).
Axes of the slice: x: 2, y: 2, z: 4, core: 2. Of those that a mesh axis runs over, the one named last changes fastest.
Arguments:
- states: bfloat16 [4, 1536, 5120], P('tm', 'group'), parts along dimension 1, may hold values from -60 to 60
- timesteps: int32 [4], P('tm'), may hold values from 0 to 999
- step_sizes: float32 [4], P('tm'), may hold values from 0.05 to 0.5
- mod_scale: float32 [5120], replicated, may hold values from -3 to 3
- mod_gate: float32 [5120], P('tensor'), may hold values from -3 to 3
- w_query: bfloat16 [5120, 3072], P('tm', 'tensor'), may hold values from -1 to 1
- w_key: bfloat16 [5120, 3072], P('tm', 'tensor'), may hold values from -1 to 1
- w_value: bfloat16 [5120, 3072], P('tm', 'tensor'), may hold values from -0.078125 to 0.078125
- query_gain: float32 [3072], P('tensor'), may hold values from 0.8 to 4.2
- key_gain: float32 [3072], P('tensor'), may hold values from 0.8 to 4.2
- w_out: bfloat16 [3072, 5120], P('tensor', 'tm'), may hold values from -0.109375 to 0.109375
Outputs:
- next_states: float32 [4, 1536, 5120], P('tm', 'group', 'tensor'), parts along dimension 1
- errors: float32 [2, 4], P('group', 'tm'), parts along dimension 0
The draws below stay inside these ranges and needn't reach their ends.
There are 2 independent parts, one for each index of `group`. The reference program is written for one: setup_inputs(seed, part) draws one part's arguments, and reference() takes and returns one part's arrays. A program takes and returns all parts, laid end to end along the dimension named above; an argument that names none is the same for every part. Nothing has to cross between parts.
All inputs are finite; a program needn't handle non-finite values.
Results may differ from the reference program's by a relative error of at most 0.0015.
Values may be sent and summed in bfloat16 or wider, within the bound.
No kernel may reach another device: no remote copies, remote signals or barrier semaphores. Data moves between devices by JAX's collectives and lax.ppermute only.
A program may use at most 128 MiB of HBM per device.

```python
import math
import jax
import jax.numpy as jnp
from jax import lax

D = 5120
HD = 128
HEADS = 24
SEQ = 768
HQ = 3072
TIMESTEPS = 4
N_TENSOR = 4


def feature_scales(low, high):
    ramp = jnp.arange(D).astype(jnp.float32) / (D - 1)
    return low * jnp.exp(ramp * jnp.log(high / low))


def draw_states(key, part):
    key = jax.random.fold_in(key, 11)
    base = jnp.clip(jax.random.normal(key, (TIMESTEPS, SEQ, D), jnp.float32), -6.0, 6.0)
    return (base * feature_scales(0.6, 1.8)).astype(jnp.bfloat16)


def draw_w_query(key, part):
    key = jax.random.fold_in(key, 21)
    own = jnp.clip(jax.random.normal(key, (D, HQ), jnp.float32), -6.0, 6.0)
    mixed = own
    return (mixed / jnp.sqrt(jnp.float32(D))).astype(jnp.bfloat16)


def draw_w_key(key, part):
    key = jax.random.fold_in(key, 22)
    own = jnp.clip(jax.random.normal(key, (D, HQ), jnp.float32), -6.0, 6.0)
    mixed = own
    return (mixed / jnp.sqrt(jnp.float32(D))).astype(jnp.bfloat16)


def draw_query_gain(key, part):
    key = jax.random.fold_in(key, 31)
    return jax.random.uniform(key, (HQ,), jnp.float32, 0.8, 1.6)


def draw_key_gain(key, part):
    key = jax.random.fold_in(key, 32)
    return jax.random.uniform(key, (HQ,), jnp.float32, 0.8, 1.6)


def place_ends(values, own_key, low, largest):
    longest = values.shape.index(max(values.shape))
    spots = []
    for shift in (0, 1):
        where = [jax.random.randint(jax.random.fold_in(own_key, axis), (), 0, length) for axis, length in enumerate(values.shape)]
        where[longest] = (where[longest] + shift) % values.shape[longest]
        spots.append(tuple(where))
    return values.at[spots[0]].set(low).at[spots[1]].set(largest)


def level_of(own_key, shape, cuts, least, largest):
    def one(position, shards_of):
        draws = jax.random.uniform(jax.random.fold_in(jax.random.fold_in(own_key, 6), position), (shards_of,), jnp.float32, least / len(cuts), largest / len(cuts))
        return jnp.repeat(jnp.exp(draws), shape[position] // shards_of).reshape((-1,) + (1,) * (len(shape) - position - 1))

    level = one(*cuts[0])
    for cut in cuts[1:]:
        level = level * one(*cut)
    return level


def noise(stream_key, dims, width, bound, pieces=(), kind=jnp.bfloat16):
    array = jax.random.normal(stream_key, dims, jnp.float32) * width
    if len(pieces) > 0:
        array = level_of(stream_key, dims, pieces, -0.22, 0.18) * array
    return jnp.clip(array, min=-bound, max=bound).astype(kind)


def setup_inputs(seed: int = 0, part: int = 0) -> dict:
    splits = jax.random.split(jax.random.key(seed), 12)
    part_keys = jax.random.split(jax.random.fold_in(splits[11], part), 12)
    return {
        "states": draw_states(jax.random.fold_in(jax.random.fold_in(splits[11], part), 71), part),
        "timesteps": place_ends(jax.random.randint(splits[1], (TIMESTEPS,), 0, 1000), jax.random.fold_in(splits[1], 1), 0, 999).astype(jnp.int32),
        "step_sizes": jnp.clip(jnp.exp(math.log(0.5) - 2.3025851 * jax.random.uniform(splits[2], (TIMESTEPS,), jnp.float32) ** level_of(splits[2], (TIMESTEPS,), ((0, 4),), -0.2, 0.2)), 0.05, 0.5),
        "mod_scale": noise(splits[3], (D,), 0.5, 3.0, (), jnp.float32),
        "mod_gate": noise(splits[4], (D,), 0.5, 3.0, ((0, 4),), jnp.float32),
        "w_query": draw_w_query(jax.random.fold_in(splits[11], 71), part),
        "w_key": draw_w_key(jax.random.fold_in(splits[11], 71), part),
        "w_value": noise(splits[7], (D, HQ), D ** -0.5, 0.078125, ((0, 4), (1, 4))),
        "query_gain": draw_query_gain(jax.random.fold_in(splits[11], 71), part),
        "key_gain": draw_key_gain(jax.random.fold_in(splits[11], 71), part),
        "w_out": noise(splits[10], (HQ, D), HQ ** -0.5, 0.109375, ((0, 4), (1, 4))),
    }


def head_norm(values, gain):
    rows = values.shape[0]
    split = values.reshape(rows, HEADS, HD)
    normed = split * lax.rsqrt(lax.optimization_barrier(jnp.mean(split * split, axis=-1, keepdims=True)) + 1e-06)
    return (normed * gain.reshape(HEADS, HD)).astype(jnp.bfloat16)

def reference(states, timesteps, step_sizes, mod_scale, mod_gate, w_query, w_key, w_value, query_gain, key_gain, w_out):
    omega = jnp.exp(-math.log(10000.0) * jnp.arange(D).astype(jnp.float32) / D)

    def one_step(packed):
        latent, stamp, step = packed
        values = latent.astype(jnp.float32)
        normed = values * lax.rsqrt(lax.optimization_barrier(jnp.mean(values * values, axis=-1, keepdims=True)) + 1e-06)
        hidden = (normed * (1.0 + mod_scale * jnp.cos(stamp * omega))).astype(jnp.bfloat16)
        query = jnp.dot(hidden, w_query, preferred_element_type=jnp.float32)
        keys = jnp.dot(hidden, w_key, preferred_element_type=jnp.float32)
        value = jnp.dot(hidden, w_value, preferred_element_type=jnp.float32)
        q_norm = head_norm(query, query_gain).astype(jnp.float32)
        k_norm = head_norm(keys, key_gain).astype(jnp.float32)
        v_heads = value.astype(jnp.bfloat16).reshape(SEQ, HEADS, HD).astype(jnp.float32)
        scores = jnp.einsum('qhd,khd->hqk', q_norm, k_norm) / math.sqrt(HD)
        probs = jax.nn.softmax(scores, axis=-1).astype(jnp.bfloat16).astype(jnp.float32)
        attended = jnp.einsum('hqk,khd->qhd', probs, v_heads).astype(jnp.bfloat16)
        grouped = attended.reshape(SEQ, N_TENSOR, HQ // N_TENSOR).astype(jnp.float32)
        out_groups = w_out.reshape(N_TENSOR, HQ // N_TENSOR, D).astype(jnp.float32)
        partials = jnp.einsum('sgh,ghd->gsd', grouped, out_groups).astype(jnp.bfloat16)
        projected = lax.optimization_barrier(jnp.sum(partials.astype(jnp.float32), axis=0))
        gate = 1.0 + mod_gate * jnp.sin(stamp * omega)
        return step * gate * projected
    terms = lax.map(one_step, (states, timesteps.astype(jnp.float32), step_sizes))
    start = states[0].astype(jnp.float32)
    totals = jnp.cumsum(terms, axis=0)
    next_states = start + totals
    before = jnp.concatenate([jnp.zeros((1, SEQ, D), jnp.float32), totals[:-1]], axis=0)
    predicted = start + before
    gap = predicted - states.astype(jnp.float32)
    errors = lax.optimization_barrier(jnp.mean(gap * gap, axis=(1, 2)))[None, :]
    return (next_states, errors)
```

```python
import functools
import math

import jax
import jax.numpy as jnp
from jax import lax
from jax.experimental import pallas as pl
from jax.experimental.pallas import tpu as pltpu
from jax.sharding import PartitionSpec as P

HD = 128
CHUNK_HEADS = 2
VMEM_LIMIT = 56 * 2**20
ANY = pl.BlockSpec(memory_space=pl.ANY)
SMEM = pl.BlockSpec(memory_space=pltpu.SMEM)
VMEM = pl.BlockSpec(memory_space=pltpu.VMEM)


def spread(block, axis, holder):
    block = jnp.where(lax.axis_index(axis) == holder, block, jnp.zeros_like(block))
    return lax.psum(block, axis)


def from_behind(array, axis, by):
    devices = lax.axis_size(axis)
    pairs = [(i, i + by) for i in range(devices) if 0 <= i + by < devices]
    return lax.ppermute(array, axis, pairs)


def head_norm(values, gain):
    rows = values.shape[0]
    count = values.shape[1] // HD
    split = values.reshape(rows, count, HD)
    normed = split * lax.rsqrt(jnp.mean(split * split, axis=-1, keepdims=True) + 1e-06)
    return (normed * gain.reshape(count, HD)).astype(jnp.bfloat16)


def make_hidden(latent, stamp, mod_scale):
    width = latent.shape[1]
    omega = jnp.exp(-math.log(10000.0) * jnp.arange(width).astype(jnp.float32) / width)
    values = latent.astype(jnp.float32)
    normed = values * lax.rsqrt(jnp.mean(values * values, axis=-1, keepdims=True) + 1e-06)
    return (normed * (1.0 + mod_scale * jnp.cos(stamp * omega))).astype(jnp.bfloat16)


def make_gate(stamp, mod_gate, width):
    share = mod_gate.shape[0]
    offset = lax.axis_index("tensor") * share
    positions = (offset + jnp.arange(share)).astype(jnp.float32)
    omega_share = jnp.exp(-math.log(10000.0) * positions / width)
    return 1.0 + mod_gate * jnp.sin(stamp * omega_share)


def general_body(
    states, timesteps, step_sizes, mod_scale, mod_gate, w_query, w_key, w_value, query_gain, key_gain, w_out
):
    latent = states[0]
    rows, width = latent.shape
    stamp = timesteps[0].astype(jnp.float32)
    hidden = make_hidden(latent, stamp, mod_scale)
    local_heads = w_query.shape[1]

    def project(weight):
        whole = lax.all_gather(weight, "tm", axis=0, tiled=True)
        return jnp.dot(hidden, whole, preferred_element_type=jnp.float32)

    count = local_heads // HD
    q_norm = head_norm(project(w_query), query_gain)
    k_norm = head_norm(project(w_key), key_gain)
    v_heads = project(w_value).astype(jnp.bfloat16).reshape(rows, count, HD)
    scores = jnp.einsum("qhd,khd->hqk", q_norm, k_norm, preferred_element_type=jnp.float32) / math.sqrt(HD)
    probs = jax.nn.softmax(scores, axis=-1).astype(jnp.bfloat16)
    attended = jnp.einsum("hqk,khd->qhd", probs, v_heads, preferred_element_type=jnp.float32)
    attended = attended.astype(jnp.bfloat16).reshape(rows, local_heads)
    share = mod_gate.shape[0]
    offset = lax.axis_index("tensor") * share
    partial_out = jnp.dot(
        attended,
        lax.all_gather(w_out, "tm", axis=1, tiled=True),
        preferred_element_type=jnp.float32,
    )
    projected = lax.psum_scatter(
        partial_out.astype(jnp.bfloat16), "tensor", scatter_dimension=1, tiled=True
    ).astype(jnp.float32)
    term = step_sizes[0] * make_gate(stamp, mod_gate, width) * projected
    own_slice = lax.dynamic_slice_in_dim(latent, offset, share, 1)
    own_start = own_slice.astype(jnp.float32)
    base_state = spread(own_slice, "tm", 0).astype(jnp.float32)
    running = term
    for level in range((lax.axis_size("tm") - 1).bit_length()):
        running = running + from_behind(running, "tm", 1 << level)
    before = running - term
    predicted = base_state + before
    next_share = predicted + term
    gap = predicted - own_start
    squared = lax.psum(jnp.sum(gap * gap), "tensor")
    errors = (squared / (rows * width)).reshape(1, 1)
    return (next_share[None], errors)


def near_kernel(idx, h_own, h_par, wq, wk, wv, pq, pk, pv, acc):
    wide = wq.shape[1]
    for n, (own, par) in enumerate(((wq, pq), (wk, pk), (wv, pv))):
        acc[0, :, n * wide : (n + 1) * wide] = jnp.dot(
            h_own[...], own[...], preferred_element_type=jnp.float32
        ) + jnp.dot(h_par[...], par[...], preferred_element_type=jnp.float32)


def near_products(hidden, own, partner, tm):
    rows, _ = hidden.shape
    depth, cols = own[0].shape
    wide = CHUNK_HEADS * HD
    chunks = cols // wide
    weight = pl.BlockSpec((depth, wide), lambda j, idx: (0, j))
    return pl.pallas_call(
        near_kernel,
        grid_spec=pltpu.PrefetchScalarGridSpec(
            num_scalar_prefetch=1,
            grid=(chunks,),
            in_specs=[
                pl.BlockSpec((rows, depth), lambda j, idx: (0, idx[0])),
                pl.BlockSpec((rows, depth), lambda j, idx: (0, idx[1])),
            ]
            + [weight] * 6,
            out_specs=pl.BlockSpec((1, rows, 3 * wide), lambda j, idx: (j, 0, 0)),
        ),
        out_shape=jax.ShapeDtypeStruct((chunks, rows, 3 * wide), jnp.float32),
        compiler_params=pltpu.CompilerParams(vmem_limit_bytes=VMEM_LIMIT),
        cost_estimate=pl.CostEstimate(
            flops=12 * rows * depth * cols, bytes_accessed=6 * depth * cols * 2, transcendentals=0
        ),
        name="near_products",
    )(jnp.stack([tm, tm ^ 1]).astype(jnp.int32), hidden, hidden, *own, *partner)


def attend_kernel(chunk, idx, hid, acc, far, far_x, par, par_x, qg, kg, out, hbuf, wbuf, abuf, sems, asem):
    rows = hbuf.shape[0]
    half = far.shape[0]
    wide = CHUNK_HEADS * HD
    pieces = (far, par, far_x, par_x)
    copies = []
    for n, piece in enumerate(pieces):
        at = pl.multiple_of(idx[n], HD)
        copies.append(
            (
                pltpu.make_async_copy(
                    hid.at[:, pl.ds(at, half)], hbuf.at[:, n * half : (n + 1) * half], sems.at[2 * n]
                ),
                pltpu.make_async_copy(piece, wbuf.at[n * half : (n + 1) * half, :], sems.at[2 * n + 1]),
            )
        )
        for copy in copies[-1]:
            copy.start()
    first = pltpu.make_async_copy(acc.at[chunk], abuf, asem)
    first.start()
    for part in range(2):
        for pair in copies[2 * part : 2 * part + 2]:
            for copy in pair:
                copy.wait()
        if part == 0:
            first.wait()
        span = slice(2 * part * half, 2 * (part + 1) * half)
        for n in range(3):
            cols = slice(n * wide, (n + 1) * wide)
            abuf[:, cols] += jnp.dot(hbuf[:, span], wbuf[span, cols], preferred_element_type=jnp.float32)

    def normed(values, gain):
        scale = lax.rsqrt(jnp.mean(values * values, axis=-1, keepdims=True) + 1e-06)
        return (values * scale * gain).astype(jnp.bfloat16)

    block = rows // 3
    for head in range(CHUNK_HEADS):
        cols = slice(head * HD, (head + 1) * HD)
        qn = normed(abuf[:, cols], qg[:, cols])
        kn = normed(abuf[:, wide + head * HD : wide + (head + 1) * HD], kg[:, cols])
        vb = abuf[:, 2 * wide + head * HD : 2 * wide + (head + 1) * HD].astype(jnp.bfloat16)
        for r in range(3):
            scores = lax.dot_general(
                qn[r * block : (r + 1) * block],
                kn,
                (((1,), (1,)), ((), ())),
                preferred_element_type=jnp.float32,
            )
            top = jnp.max(scores, axis=-1, keepdims=True)
            grown = jnp.exp((scores - top) * (1.0 / math.sqrt(HD)))
            probs = grown * (1.0 / jnp.sum(grown, axis=-1, keepdims=True))
            out[r * block : (r + 1) * block, cols] = jnp.dot(
                probs.astype(jnp.bfloat16), vb, preferred_element_type=jnp.float32
            ).astype(jnp.bfloat16)


def attend(chunk, idx, hidden, acc, pieces, qg, kg):
    rows = hidden.shape[0]
    half = pieces[0].shape[0]
    wide = CHUNK_HEADS * HD
    gains = [g.reshape(1, -1)[:, chunk * wide : (chunk + 1) * wide] for g in (qg, kg)]
    return pl.pallas_call(
        functools.partial(attend_kernel, chunk),
        in_specs=[SMEM] + [ANY] * 6 + [VMEM] * 2,
        out_specs=VMEM,
        out_shape=jax.ShapeDtypeStruct((rows, wide), jnp.bfloat16),
        scratch_shapes=[
            pltpu.VMEM((rows, 4 * half), jnp.bfloat16),
            pltpu.VMEM((4 * half, 3 * wide), jnp.bfloat16),
            pltpu.VMEM((rows, 3 * wide), jnp.float32),
            pltpu.SemaphoreType.DMA((8,)),
            pltpu.SemaphoreType.DMA,
        ],
        compiler_params=pltpu.CompilerParams(vmem_limit_bytes=VMEM_LIMIT),
        cost_estimate=pl.CostEstimate(
            flops=2 * rows * 4 * half * 3 * wide * 2, bytes_accessed=12 * 2**20, transcendentals=CHUNK_HEADS * rows * rows
        ),
        name="attend",
    )(idx, hidden, acc, *pieces, *gains)


def out_kernel(devices, chunks, idx, gate, *refs):
    own, refs = refs[:chunks], refs[chunks:]
    right, refs = refs[: (devices - 1) * chunks], refs[(devices - 1) * chunks :]
    left, refs = refs[: (devices - 1) * chunks], refs[(devices - 1) * chunks :]
    held, refs = refs[:devices], refs[devices:]
    held_x, refs = refs[:devices], refs[devices:]
    given, refs = refs[:devices], refs[devices:]
    given_x, refs = refs[:devices], refs[devices:]
    out, att, w, asems, wsems = refs
    wide = own[0].shape[1]
    half = held[0].shape[0]
    z, source, g = idx[0], idx[1], idx[2]
    waits = []
    for d in range(devices):
        here = []
        for j in range(chunks):
            place = att.at[d, :, j * wide : (j + 1) * wide]
            if d == 0:
                pltpu.make_async_copy(own[j], place, asems.at[d * chunks + j]).start()
            else:
                behind = z + d >= devices

                @pl.when(behind)
                def _(d=d, j=j, place=place):
                    pltpu.make_async_copy(
                        right[(devices - d - 1) * chunks + j], place, asems.at[d * chunks + j]
                    ).start()

                @pl.when(jnp.logical_not(behind))
                def _(d=d, j=j, place=place):
                    pltpu.make_async_copy(left[(d - 1) * chunks + j], place, asems.at[d * chunks + j]).start()

            here.append(pltpu.make_async_copy(own[j], place, asems.at[d * chunks + j]))
        for n, (mine, other) in enumerate(((held, given), (held_x, given_x))):
            at = pl.multiple_of((g if n == 0 else 1 - g) * half, 16)
            place = w.at[d, pl.ds(at, half), :]

            @pl.when(source == 1)
            def _(d=d, n=n, place=place, mine=mine):
                pltpu.make_async_copy(mine[d], place, wsems.at[2 * d + n]).start()

            @pl.when(source == 0)
            def _(d=d, n=n, place=place, other=other):
                pltpu.make_async_copy(other[d], place, wsems.at[2 * d + n]).start()

            here.append(pltpu.make_async_copy(mine[d], place, wsems.at[2 * d + n]))
        waits.append(here)
    share = out.shape[1]
    block = 256 if share % 256 == 0 else share
    for d in range(devices):
        for copy in waits[d]:
            copy.wait()
        for n in range(share // block):
            cols = slice(n * block, (n + 1) * block)
            part = (
                jnp.dot(att[d], w[d, :, cols], preferred_element_type=jnp.float32)
                .astype(jnp.bfloat16)
                .astype(jnp.float32)
            )
            if d > 0:
                part = out[:, cols] + part
            if d == devices - 1:
                part = gate[:, cols] * part
            out[:, cols] = part


def out_projection(idx, gate, own, right, left, held, held_x, given, given_x):
    chunks = len(own)
    devices = len(held)
    rows, wide = own[0].shape
    half, share = held[0].shape
    operands = (*own, *right, *left, *held, *held_x, *given, *given_x)
    return pl.pallas_call(
        functools.partial(out_kernel, devices, chunks),
        in_specs=[SMEM, VMEM] + [ANY] * len(operands),
        out_specs=VMEM,
        out_shape=jax.ShapeDtypeStruct((rows, share), jnp.float32),
        scratch_shapes=[
            pltpu.VMEM((devices, rows, chunks * wide), jnp.bfloat16),
            pltpu.VMEM((devices, 2 * half, share), jnp.bfloat16),
            pltpu.SemaphoreType.DMA((devices * chunks,)),
            pltpu.SemaphoreType.DMA((2 * devices,)),
        ],
        compiler_params=pltpu.CompilerParams(vmem_limit_bytes=VMEM_LIMIT),
        cost_estimate=pl.CostEstimate(
            flops=2 * rows * devices * chunks * wide * share * 2, bytes_accessed=18 * 2**20, transcendentals=0
        ),
        name="out_projection",
    )(idx, gate, *operands)


def fast_body(
    states, timesteps, step_sizes, mod_scale, mod_gate, w_query, w_key, w_value, query_gain, key_gain, w_out
):
    latent = states[0]
    rows, width = latent.shape
    stamp = timesteps[0].astype(jnp.float32)
    g, t, z = lax.axis_index("group"), lax.axis_index("tm"), lax.axis_index("tensor")
    steps, devices = lax.axis_size("tm"), lax.axis_size("tensor")
    depth, cols = w_query.shape
    half = depth // 2
    wide = CHUNK_HEADS * HD
    chunks = cols // wide

    def over(array, axis, flip):
        return lax.ppermute(array, axis, [(i, i ^ flip) for i in range(lax.axis_size(axis))])

    def plane(array, pairs):
        flat = [(a[0] * devices + a[1], b[0] * devices + b[1]) for a, b in pairs]
        return lax.ppermute(array, ("tm", "tensor"), flat)

    sends = []
    for j in range(chunks):
        parts = [
            lax.dynamic_slice(w, (g * half, j * wide), (half, wide)) for w in (w_query, w_key, w_value)
        ]
        sends.append(jnp.concatenate(parts, axis=1))
    far = [over(s, "tm", 2) for s in sends]
    partner = [over(w, "tm", 1) for w in (w_query, w_key, w_value)]

    w_rows = w_out.shape[0] // 2
    own_half = lax.dynamic_slice_in_dim(w_out, g * w_rows, w_rows, 0)
    sent = [own_half] + [
        plane(own_half, [((s, (s + d) % devices), (s, s)) for s in range(steps)]) for d in range(1, devices)
    ]

    hidden = make_hidden(latent, stamp, mod_scale)
    acc = near_products(hidden, (w_query, w_key, w_value), partner, t)
    at_far, at_par = (t ^ 2) * depth, (t ^ 3) * depth
    idx = jnp.stack([at_far + g * half, at_par + g * half, at_far + (1 - g) * half, at_par + (1 - g) * half])
    idx = idx.astype(jnp.int32)

    far_x = [over(f, "group", 1) for f in far]
    par = [over(f, "tm", 1) for f in far]
    par_x = [over(f, "tm", 1) for f in far_x]

    own = []
    right = [[] for _ in range(devices - 1)]
    left = [[] for _ in range(devices - 1)]
    for j in range(chunks):
        att = attend(j, idx, hidden, acc, (far[j], far_x[j], par[j], par_x[j]), query_gain, key_gain)
        own.append(att)
        up = down = att
        for d in range(1, devices):
            up = lax.ppermute(up, "tensor", [(i, i + 1) for i in range(d - 1, devices - 1)])
            down = lax.ppermute(down, "tensor", [(i + 1, i) for i in range(0, devices - d)])
            right[d - 1].append(up)
            left[d - 1].append(down)

    across = [plane(s, [((s_, s_), (s_ ^ 2, s_)) for s_ in range(steps)]) for s in sent]
    held = [jnp.where(t == z, s, a) for s, a in zip(sent, across)]
    held_x = [over(h, "group", 1) for h in held]
    to_core = [((s, s), (s ^ 1, s)) for s in range(steps)] + [((s ^ 2, s), (s ^ 3, s)) for s in range(steps)]
    given = [plane(h, to_core) for h in held]
    given_x = [plane(h, to_core) for h in held_x]

    share = mod_gate.shape[0]
    gate = (step_sizes[0] * make_gate(stamp, mod_gate, width)).reshape(1, share)
    source = jnp.logical_or(t == z, t == (z ^ 2))
    out_idx = jnp.stack([z, source.astype(jnp.int32), g]).astype(jnp.int32)
    flat = lambda lists: [b for one in lists for b in one]
    term = out_projection(out_idx, gate, own, flat(right), flat(left), held, held_x, given, given_x)

    own_slice = lax.dynamic_slice_in_dim(latent, z * share, share, 1)
    start_core = lax.ppermute(own_slice, "tm", [(0, 1)])
    start_far = lax.ppermute(own_slice, "tm", [(0, 2)])
    start_last = lax.ppermute(start_far, "tm", [(2, 3)])
    start = jnp.where(t == 0, own_slice, jnp.where(t == 1, start_core, jnp.where(t == 2, start_far, start_last)))
    start = start.astype(jnp.float32)

    odd = t % 2 == 1
    before_core = lax.ppermute(term, "tm", [(0, 1), (2, 3)])
    chip_sum = before_core + term
    carry_last = lax.ppermute(chip_sum, "tm", [(1, 3)])
    carry_far = lax.ppermute(carry_last, "tm", [(3, 2)])
    before = jnp.where(odd, before_core, 0.0) + jnp.where(t == 2, carry_far, jnp.where(t == 3, carry_last, 0.0))
    predicted = start + before
    next_share = predicted + term
    gap = predicted - own_slice.astype(jnp.float32)
    squared = lax.psum(jnp.sum(gap * gap), "tensor")
    errors = (squared / (rows * width)).reshape(1, 1)
    return (next_share[None], errors)


def solution(mesh):
    placed = (
        P("tm", "group", None),
        P("tm"),
        P("tm"),
        P(),
        P("tensor"),
        P("tm", "tensor"),
        P("tm", "tensor"),
        P("tm", "tensor"),
        P("tensor"),
        P("tensor"),
        P("tensor", "tm"),
    )
    fast = mesh.shape["group"] == 2 and mesh.shape["tm"] == 4 and mesh.shape["tensor"] == 4
    return jax.shard_map(
        fast_body if fast else general_body,
        mesh=mesh,
        in_specs=placed,
        out_specs=(P("tm", "group", "tensor"), P("group", "tm")),
        check_vma=False,
    )
```

```python
import functools
import math

import jax
import jax.numpy as jnp
from jax import lax
from jax.experimental import pallas as pl
from jax.experimental.pallas import tpu as pltpu
from jax.sharding import PartitionSpec as P

HD = 128
CHUNK_HEADS = 2
PARTS = 2
CARRY = jnp.bfloat16
COST = 1e6
VMEM_LIMIT = 56 * 2**20
ANY = pl.BlockSpec(memory_space=pl.ANY)
SMEM = pl.BlockSpec(memory_space=pltpu.SMEM)
VMEM = pl.BlockSpec(memory_space=pltpu.VMEM)


def spread(block, axis, holder):
    block = jnp.where(lax.axis_index(axis) == holder, block, jnp.zeros_like(block))
    return lax.psum(block, axis)


def from_behind(array, axis, by):
    devices = lax.axis_size(axis)
    pairs = [(i, i + by) for i in range(devices) if 0 <= i + by < devices]
    return lax.ppermute(array, axis, pairs)


def head_norm(values, gain):
    rows = values.shape[0]
    count = values.shape[1] // HD
    split = values.reshape(rows, count, HD)
    normed = split * lax.rsqrt(jnp.mean(split * split, axis=-1, keepdims=True) + 1e-06)
    return (normed * gain.reshape(count, HD)).astype(jnp.bfloat16)


def make_hidden(latent, stamp, mod_scale):
    width = latent.shape[1]
    omega = jnp.exp(-math.log(10000.0) * jnp.arange(width).astype(jnp.float32) / width)
    values = latent.astype(jnp.float32)
    normed = values * lax.rsqrt(jnp.mean(values * values, axis=-1, keepdims=True) + 1e-06)
    return (normed * (1.0 + mod_scale * jnp.cos(stamp * omega))).astype(jnp.bfloat16)


def make_gate(stamp, mod_gate, width):
    share = mod_gate.shape[0]
    offset = lax.axis_index("tensor") * share
    positions = (offset + jnp.arange(share)).astype(jnp.float32)
    omega_share = jnp.exp(-math.log(10000.0) * positions / width)
    return 1.0 + mod_gate * jnp.sin(stamp * omega_share)


def general_body(
    states, timesteps, step_sizes, mod_scale, mod_gate, w_query, w_key, w_value, query_gain, key_gain, w_out
):
    latent = states[0]
    rows, width = latent.shape
    stamp = timesteps[0].astype(jnp.float32)
    hidden = make_hidden(latent, stamp, mod_scale)
    local_heads = w_query.shape[1]

    def project(weight):
        whole = lax.all_gather(weight, "tm", axis=0, tiled=True)
        return jnp.dot(hidden, whole, preferred_element_type=jnp.float32)

    count = local_heads // HD
    q_norm = head_norm(project(w_query), query_gain)
    k_norm = head_norm(project(w_key), key_gain)
    v_heads = project(w_value).astype(jnp.bfloat16).reshape(rows, count, HD)
    scores = jnp.einsum("qhd,khd->hqk", q_norm, k_norm, preferred_element_type=jnp.float32) / math.sqrt(HD)
    probs = jax.nn.softmax(scores, axis=-1).astype(jnp.bfloat16)
    attended = jnp.einsum("hqk,khd->qhd", probs, v_heads, preferred_element_type=jnp.float32)
    attended = attended.astype(jnp.bfloat16).reshape(rows, local_heads)
    share = mod_gate.shape[0]
    offset = lax.axis_index("tensor") * share
    partial_out = jnp.dot(
        attended,
        lax.all_gather(w_out, "tm", axis=1, tiled=True),
        preferred_element_type=jnp.float32,
    )
    projected = lax.psum_scatter(
        partial_out.astype(jnp.bfloat16), "tensor", scatter_dimension=1, tiled=True
    ).astype(jnp.float32)
    term = step_sizes[0] * make_gate(stamp, mod_gate, width) * projected
    own_slice = lax.dynamic_slice_in_dim(latent, offset, share, 1)
    own_start = own_slice.astype(jnp.float32)
    base_state = spread(own_slice, "tm", 0).astype(jnp.float32)
    running = term
    for level in range((lax.axis_size("tm") - 1).bit_length()):
        running = running + from_behind(running, "tm", 1 << level)
    before = running - term
    predicted = base_state + before
    next_share = predicted + term
    gap = predicted - own_start
    squared = lax.psum(jnp.sum(gap * gap), "tensor")
    errors = (squared / (rows * width)).reshape(1, 1)
    return (next_share[None], errors)


def after(value, *others):
    return lax.optimization_barrier((value, *others))[0]


def hidden_kernel(latent, scale, out):
    values = latent[0].astype(jnp.float32)
    normed = values * lax.rsqrt(jnp.mean(values * values, axis=-1, keepdims=True) + 1e-06)
    out[...] = (normed * scale[...]).astype(jnp.bfloat16)


def fast_hidden(states, stamp, mod_scale):
    _, rows, width = states.shape
    omega = jnp.exp(-math.log(10000.0) * jnp.arange(width).astype(jnp.float32) / width)
    scale = (1.0 + mod_scale * jnp.cos(stamp * omega)).reshape(1, width)
    block = 96 if rows % 96 == 0 else rows
    return pl.pallas_call(
        hidden_kernel,
        grid=(rows // block,),
        in_specs=[
            pl.BlockSpec((1, block, width), lambda i: (0, i, 0)),
            pl.BlockSpec((1, width), lambda i: (0, 0)),
        ],
        out_specs=pl.BlockSpec((block, width), lambda i: (i, 0)),
        out_shape=jax.ShapeDtypeStruct((rows, width), jnp.bfloat16),
        compiler_params=pltpu.CompilerParams(vmem_limit_bytes=VMEM_LIMIT),
        cost_estimate=cost(5),
        name="hidden",
    )(states, scale)


def phase(*values):
    return lax.optimization_barrier(values)


def cost(micros):
    return pl.CostEstimate(flops=int(micros * 1e3 * COST), bytes_accessed=1024, transcendentals=0)


def pack_kernel(idx, wq, wk, wv, out):
    wide = wq.shape[1]
    for n, w in enumerate((wq, wk, wv)):
        out[:, n * wide : (n + 1) * wide] = w[...]


def pack(chunk, group, weights):
    depth = weights[0].shape[0]
    wide = CHUNK_HEADS * HD
    blocks = 2
    tall = depth // 2 // blocks
    return pl.pallas_call(
        pack_kernel,
        grid_spec=pltpu.PrefetchScalarGridSpec(
            num_scalar_prefetch=1,
            grid=(blocks,),
            in_specs=[pl.BlockSpec((tall, wide), lambda i, idx: (idx[0] * blocks + i, chunk))] * 3,
            out_specs=pl.BlockSpec((tall, 3 * wide), lambda i, idx: (i, 0)),
        ),
        out_shape=jax.ShapeDtypeStruct((depth // 2, 3 * wide), jnp.bfloat16),
        cost_estimate=cost(1),
        name="pack",
    )(group.astype(jnp.int32).reshape(1), *weights)


def near_kernel(idx, h_own, h_par, wq, wk, wv, pq, pk, pv, acc):
    wide = wq.shape[1]
    for n, (own, par) in enumerate(((wq, pq), (wk, pk), (wv, pv))):
        acc[0, :, n * wide : (n + 1) * wide] = jnp.dot(
            h_own[...], own[...], preferred_element_type=jnp.float32
        ) + jnp.dot(h_par[...], par[...], preferred_element_type=jnp.float32)


def near_products(hidden, own, partner, tm):
    rows, _ = hidden.shape
    depth, cols = own[0].shape
    wide = CHUNK_HEADS * HD
    chunks = cols // wide
    weight = pl.BlockSpec((depth, wide), lambda j, idx: (0, j))
    return pl.pallas_call(
        near_kernel,
        grid_spec=pltpu.PrefetchScalarGridSpec(
            num_scalar_prefetch=1,
            grid=(chunks,),
            in_specs=[
                pl.BlockSpec((rows, depth), lambda j, idx: (0, idx[0])),
                pl.BlockSpec((rows, depth), lambda j, idx: (0, idx[1])),
            ]
            + [weight] * 6,
            out_specs=pl.BlockSpec((1, rows, 3 * wide), lambda j, idx: (j, 0, 0)),
        ),
        out_shape=jax.ShapeDtypeStruct((chunks, rows, 3 * wide), jnp.float32),
        compiler_params=pltpu.CompilerParams(vmem_limit_bytes=VMEM_LIMIT),
        cost_estimate=cost(15),
        name="near_products",
    )(jnp.stack([tm, tm ^ 1]).astype(jnp.int32), hidden, hidden, *own, *partner)


def attend_kernel(chunk, idx, hid, acc, far, far_x, par, par_x, qg, kg, out, hbuf, wbuf, abuf, sems, asem):
    rows = hbuf.shape[0]
    half = far.shape[0]
    wide = CHUNK_HEADS * HD
    pieces = (far, par, far_x, par_x)
    copies = []
    for n, piece in enumerate(pieces):
        at = pl.multiple_of(idx[n], HD)
        copies.append(
            (
                pltpu.make_async_copy(
                    hid.at[:, pl.ds(at, half)], hbuf.at[:, n * half : (n + 1) * half], sems.at[2 * n]
                ),
                pltpu.make_async_copy(piece, wbuf.at[n * half : (n + 1) * half, :], sems.at[2 * n + 1]),
            )
        )
        for copy in copies[-1]:
            copy.start()
    first = pltpu.make_async_copy(acc.at[chunk], abuf, asem)
    first.start()
    for part in range(2):
        for pair in copies[2 * part : 2 * part + 2]:
            for copy in pair:
                copy.wait()
        if part == 0:
            first.wait()
        span = slice(2 * part * half, 2 * (part + 1) * half)
        for n in range(3):
            cols = slice(n * wide, (n + 1) * wide)
            abuf[:, cols] += jnp.dot(hbuf[:, span], wbuf[span, cols], preferred_element_type=jnp.float32)

    def normed(values, gain):
        scale = lax.rsqrt(jnp.mean(values * values, axis=-1, keepdims=True) + 1e-06)
        return (values * scale * gain).astype(jnp.bfloat16)

    block = rows // 3
    for head in range(CHUNK_HEADS):
        cols = slice(head * HD, (head + 1) * HD)
        qn = normed(abuf[:, cols], qg[:, cols])
        kn = normed(abuf[:, wide + head * HD : wide + (head + 1) * HD], kg[:, cols])
        vb = abuf[:, 2 * wide + head * HD : 2 * wide + (head + 1) * HD].astype(jnp.bfloat16)
        for r in range(3):
            scores = lax.dot_general(
                qn[r * block : (r + 1) * block],
                kn,
                (((1,), (1,)), ((), ())),
                preferred_element_type=jnp.float32,
            )
            top = jnp.max(scores, axis=-1, keepdims=True)
            grown = jnp.exp((scores - top) * (1.0 / math.sqrt(HD)))
            probs = grown * (1.0 / jnp.sum(grown, axis=-1, keepdims=True))
            out[r * block : (r + 1) * block, cols] = jnp.dot(
                probs.astype(jnp.bfloat16), vb, preferred_element_type=jnp.float32
            ).astype(jnp.bfloat16)


def attend(chunk, idx, hidden, acc, pieces, qg, kg):
    rows = hidden.shape[0]
    half = pieces[0].shape[0]
    wide = CHUNK_HEADS * HD
    gains = [g.reshape(1, -1)[:, chunk * wide : (chunk + 1) * wide] for g in (qg, kg)]
    return pl.pallas_call(
        functools.partial(attend_kernel, chunk),
        in_specs=[SMEM] + [ANY] * 6 + [VMEM] * 2,
        out_specs=VMEM,
        out_shape=jax.ShapeDtypeStruct((rows, wide), jnp.bfloat16),
        scratch_shapes=[
            pltpu.VMEM((rows, 4 * half), jnp.bfloat16),
            pltpu.VMEM((4 * half, 3 * wide), jnp.bfloat16),
            pltpu.VMEM((rows, 3 * wide), jnp.float32),
            pltpu.SemaphoreType.DMA((8,)),
            pltpu.SemaphoreType.DMA,
        ],
        compiler_params=pltpu.CompilerParams(vmem_limit_bytes=VMEM_LIMIT),
        cost_estimate=cost(12),
        name="attend",
    )(idx, hidden, acc, *pieces, *gains)


def out_kernel(devices, chunks, top, idx, gate, *refs):
    gathered, pieces, (out, att, w, asems, wsems) = refs[:chunks], refs[chunks : chunks + 8], refs[chunks + 8 :]
    rows = out.shape[0]
    wide = gathered[0].shape[2]
    half = pieces[0].shape[0]
    core, g = idx[0], idx[1]
    waits = []
    for d in range(devices):
        here = []
        for j in range(chunks):
            here.append(
                pltpu.make_async_copy(
                    gathered[j].at[d, top : top + rows],
                    att.at[d, :, j * wide : (j + 1) * wide],
                    asems.at[d * chunks + j],
                )
            )
            here[-1].start()
        waits.append(here)
    wcopies = []
    for n, piece in enumerate(pieces):
        lower, other, swap = n // 4, (n // 2) % 2, n % 2
        block = 2 * (core if other == 0 else 1 - core) + (g if swap == 0 else 1 - g)
        place = w.at[block, lower * half : (lower + 1) * half, :]
        wcopies.append(pltpu.make_async_copy(piece, place, wsems.at[n]))
        wcopies[-1].start()
    share = out.shape[1]
    block = 256 if share % 256 == 0 else share
    for d in range(devices):
        for copy in waits[d]:
            copy.wait()
        if d == 0:
            for copy in wcopies:
                copy.wait()
        for n in range(share // block):
            cols = slice(n * block, (n + 1) * block)
            part = (
                jnp.dot(att[d], w[d, :, cols], preferred_element_type=jnp.float32)
                .astype(jnp.bfloat16)
                .astype(jnp.float32)
            )
            if d > 0:
                part = out[:, cols] + part
            if d == devices - 1:
                part = gate[:, cols] * part
            out[:, cols] = part


def out_projection(top, count, idx, gate, gathered, pieces):
    chunks = len(gathered)
    devices, rows, wide = gathered[0].shape
    half, share = pieces[0].shape
    return pl.pallas_call(
        functools.partial(out_kernel, devices, chunks, top),
        in_specs=[SMEM, VMEM] + [ANY] * (chunks + 8),
        out_specs=VMEM,
        out_shape=jax.ShapeDtypeStruct((count, share), jnp.float32),
        scratch_shapes=[
            pltpu.VMEM((devices, count, chunks * wide), jnp.bfloat16),
            pltpu.VMEM((devices, 2 * half, share), jnp.bfloat16),
            pltpu.SemaphoreType.DMA((devices * chunks,)),
            pltpu.SemaphoreType.DMA((8,)),
        ],
        compiler_params=pltpu.CompilerParams(vmem_limit_bytes=VMEM_LIMIT),
        cost_estimate=cost(7),
        name="out_projection",
    )(idx, gate, *gathered, *pieces)


def fast_body(
    states, timesteps, step_sizes, mod_scale, mod_gate, w_query, w_key, w_value, query_gain, key_gain, w_out
):
    latent = states[0]
    rows, width = latent.shape
    stamp = timesteps[0].astype(jnp.float32)
    g, t, z = lax.axis_index("group"), lax.axis_index("tm"), lax.axis_index("tensor")
    devices = 4
    depth, cols = w_query.shape
    half = depth // 2
    chunks = cols // (CHUNK_HEADS * HD)

    def over(array, axis, flip):
        return lax.ppermute(array, axis, [(i, i ^ flip) for i in range(lax.axis_size(axis))])

    weights = (w_query, w_key, w_value)
    sends = [pack(0, g, weights)]
    for j in range(1, chunks):
        sends.append(pack(j, g, (after(weights[0], sends[-1]), *weights[1:])))
    at_far, at_par = (t ^ 2) * depth, (t ^ 3) * depth
    idx = jnp.stack([at_far + g * half, at_par + g * half, at_far + (1 - g) * half, at_par + (1 - g) * half])
    idx = idx.astype(jnp.int32)
    share = mod_gate.shape[0]
    steps = range(4)

    def place(group, step, tensor):
        return (group * 4 + step) * devices + tensor

    def far(array):
        return over(array, "tm", 2)

    def swap(array):
        return over(array, "group", 1)

    def partner(array):
        return over(array, "tm", 1)

    def attended(j, acc, pieces):
        return attend(j, idx, hidden, acc, pieces, query_gain, key_gain)

    y0 = far(sends[0])
    to_plane = [
        (place(b % 2, a, b), place(b % 2, 2 * (a // 2) + b // 2, a)) for a in steps for b in range(devices)
    ]
    sent = lax.ppermute(w_out, ("group", "tm", "tensor"), to_plane)
    pq, pk, pv = (partner(w) for w in weights)
    hidden = fast_hidden(after(states, *sends), stamp, mod_scale)
    y0, pq, pk, pv, hidden, s1, s2 = phase(y0, pq, pk, pv, hidden, sends[1], sends[2])

    y1, x0, c0 = far(s1), swap(y0), partner(y0)
    acc = near_products(hidden, weights, (pq, pk, pv), t)
    y1, x0, c0, acc, s2, sent = phase(y1, x0, c0, acc, s2, sent)

    y2, x1, c1 = far(s2), swap(y1), partner(y1)
    att0 = attended(0, acc, (y0, x0, c0, partner(x0)))
    y2, x1, c1, att0, sent = phase(y2, x1, c1, att0, sent)

    w_rows = w_out.shape[0] // 2
    home = (t // 2) == (z // 2)
    upper, lower = sent[:w_rows], sent[w_rows:]
    crossing = [(a * devices + b, (a ^ 2) * devices + b) for a in steps for b in range(devices) if a // 2 == b // 2]

    def cross(array):
        return lax.ppermute(array, ("tm", "tensor"), crossing)

    g0 = lax.all_gather(att0, "tensor")
    u, x2, c2 = cross(upper), swap(y2), partner(y2)
    att1 = attended(1, acc, (y1, x1, c1, partner(x1)))
    u, x2, c2, att1, sent = phase(u, x2, c2, att1, sent)

    g1 = lax.all_gather(att1, "tensor")
    upper, lower = sent[:w_rows], sent[w_rows:]
    v = jnp.where(home, upper, u)
    w, xv, cv = cross(lower), swap(v), partner(v)
    att2 = attended(2, acc, (y2, x2, c2, partner(x2)))
    w, xv, cv, att2, v, sent = phase(w, xv, cv, att2, v, sent)

    g2 = lax.all_gather(att2, "tensor")
    lower = sent[w_rows:]
    w = jnp.where(home, lower, w)
    own_slice = lax.dynamic_slice_in_dim(latent, z * share, share, 1)
    xw, cw, cxv = swap(w), partner(w), partner(xv)
    start_far = lax.ppermute(own_slice, "tm", [(0, 2)])
    start_core = lax.ppermute(own_slice, "tm", [(0, 1)])
    xw, cw, cxv, start_far, start_core = phase(xw, cw, cxv, start_far, start_core)
    start_last = lax.ppermute(start_far, "tm", [(2, 3)])
    pieces = [v, xv, cv, cxv, w, xw, cw, partner(xw)]
    gathered = [g0, g1, g2]

    gate = (step_sizes[0] * make_gate(stamp, mod_gate, width)).reshape(1, share)
    gate = after(gate, start_core, start_last)
    out_idx = jnp.stack([t % 2, g]).astype(jnp.int32)
    odd = t % 2 == 1
    count = rows // PARTS
    terms, befores = [], []
    last = None
    for r in range(PARTS):
        feed = gate if last is None else after(gate, last)
        term = out_projection(r * count, count, out_idx, feed, gathered, pieces)
        last = term
        before_core = lax.ppermute(term, "tm", [(0, 1), (2, 3)])
        chip_sum = (before_core + term).astype(CARRY)
        carry_last = lax.ppermute(chip_sum, "tm", [(1, 3)])
        carry_far = lax.ppermute(carry_last, "tm", [(3, 2)])
        carry = jnp.where(t == 2, carry_far, jnp.where(t == 3, carry_last, jnp.zeros_like(carry_last)))
        terms.append(term)
        befores.append(jnp.where(odd, before_core, 0.0) + carry.astype(jnp.float32))
    start = jnp.where(t == 0, own_slice, jnp.where(t == 1, start_core, jnp.where(t == 2, start_far, start_last)))
    predicted = start.astype(jnp.float32) + jnp.concatenate(befores)
    next_share = predicted + jnp.concatenate(terms)
    gap = predicted - own_slice.astype(jnp.float32)
    squared = lax.psum(jnp.sum(gap * gap), "tensor")
    errors = (squared / (rows * width)).reshape(1, 1)
    return (next_share[None], errors)


def solution(mesh):
    placed = (
        P("tm", "group", None),
        P("tm"),
        P("tm"),
        P(),
        P("tensor"),
        P("tm", "tensor"),
        P("tm", "tensor"),
        P("tm", "tensor"),
        P("tensor"),
        P("tensor"),
        P("tensor", "tm"),
    )
    fast = mesh.shape["group"] == 2 and mesh.shape["tm"] == 4 and mesh.shape["tensor"] == 4
    return jax.shard_map(
        fast_body if fast else general_body,
        mesh=mesh,
        in_specs=placed,
        out_specs=(P("tm", "group", "tensor"), P("group", "tm")),
        check_vma=False,
    )
```

```python
import functools
import math

import jax
import jax.numpy as jnp
from jax import lax
from jax.experimental import pallas as pl
from jax.experimental.pallas import tpu as pltpu
from jax.sharding import PartitionSpec as P

HD = 128
CARRY = jnp.bfloat16
COST = 1e6
VMEM_LIMIT = 56 * 2**20
ANY = pl.BlockSpec(memory_space=pltpu.HBM)
SMEM = pl.BlockSpec(memory_space=pltpu.SMEM)
VMEM = pl.BlockSpec(memory_space=pltpu.VMEM)


def spread(block, axis, holder):
    block = jnp.where(lax.axis_index(axis) == holder, block, jnp.zeros_like(block))
    return lax.psum(block, axis)


def from_behind(array, axis, by):
    devices = lax.axis_size(axis)
    pairs = [(i, i + by) for i in range(devices) if 0 <= i + by < devices]
    return lax.ppermute(array, axis, pairs)


def head_norm(values, gain):
    rows = values.shape[0]
    count = values.shape[1] // HD
    split = values.reshape(rows, count, HD)
    normed = split * lax.rsqrt(jnp.mean(split * split, axis=-1, keepdims=True) + 1e-06)
    return (normed * gain.reshape(count, HD)).astype(jnp.bfloat16)


def make_hidden(latent, stamp, mod_scale):
    width = latent.shape[1]
    omega = jnp.exp(-math.log(10000.0) * jnp.arange(width).astype(jnp.float32) / width)
    values = latent.astype(jnp.float32)
    normed = values * lax.rsqrt(jnp.mean(values * values, axis=-1, keepdims=True) + 1e-06)
    return (normed * (1.0 + mod_scale * jnp.cos(stamp * omega))).astype(jnp.bfloat16)


def make_gate(stamp, mod_gate, width):
    share = mod_gate.shape[0]
    offset = lax.axis_index("tensor") * share
    positions = (offset + jnp.arange(share)).astype(jnp.float32)
    omega_share = jnp.exp(-math.log(10000.0) * positions / width)
    return 1.0 + mod_gate * jnp.sin(stamp * omega_share)


def general_body(
    states, timesteps, step_sizes, mod_scale, mod_gate, w_query, w_key, w_value, query_gain, key_gain, w_out
):
    latent = states[0]
    rows, width = latent.shape
    stamp = timesteps[0].astype(jnp.float32)
    hidden = make_hidden(latent, stamp, mod_scale)
    local_heads = w_query.shape[1]

    def project(weight):
        whole = lax.all_gather(weight, "tm", axis=0, tiled=True)
        return jnp.dot(hidden, whole, preferred_element_type=jnp.float32)

    count = local_heads // HD
    q_norm = head_norm(project(w_query), query_gain)
    k_norm = head_norm(project(w_key), key_gain)
    v_heads = project(w_value).astype(jnp.bfloat16).reshape(rows, count, HD)
    scores = jnp.einsum("qhd,khd->hqk", q_norm, k_norm, preferred_element_type=jnp.float32) / math.sqrt(HD)
    probs = jax.nn.softmax(scores, axis=-1).astype(jnp.bfloat16)
    attended = jnp.einsum("hqk,khd->qhd", probs, v_heads, preferred_element_type=jnp.float32)
    attended = attended.astype(jnp.bfloat16).reshape(rows, local_heads)
    share = mod_gate.shape[0]
    offset = lax.axis_index("tensor") * share
    partial_out = jnp.dot(
        attended,
        lax.all_gather(w_out, "tm", axis=1, tiled=True),
        preferred_element_type=jnp.float32,
    )
    projected = lax.psum_scatter(
        partial_out.astype(jnp.bfloat16), "tensor", scatter_dimension=1, tiled=True
    ).astype(jnp.float32)
    term = step_sizes[0] * make_gate(stamp, mod_gate, width) * projected
    own_slice = lax.dynamic_slice_in_dim(latent, offset, share, 1)
    own_start = own_slice.astype(jnp.float32)
    base_state = spread(own_slice, "tm", 0).astype(jnp.float32)
    running = term
    for level in range((lax.axis_size("tm") - 1).bit_length()):
        running = running + from_behind(running, "tm", 1 << level)
    before = running - term
    predicted = base_state + before
    next_share = predicted + term
    gap = predicted - own_start
    squared = lax.psum(jnp.sum(gap * gap), "tensor")
    errors = (squared / (rows * width)).reshape(1, 1)
    return (next_share[None], errors)


def after(value, *others):
    return lax.optimization_barrier((value, *others))[0]


def hidden_kernel(latent, scale, out):
    values = latent[0].astype(jnp.float32)
    normed = values * lax.rsqrt(jnp.mean(values * values, axis=-1, keepdims=True) + 1e-06)
    out[...] = (normed * scale[...]).astype(jnp.bfloat16)


def make_scale(stamp, mod_scale):
    width = mod_scale.shape[0]
    omega = jnp.exp(-math.log(10000.0) * jnp.arange(width).astype(jnp.float32) / width)
    return (1.0 + mod_scale * jnp.cos(stamp * omega)).reshape(1, width)


def fast_hidden(states, scale):
    _, rows, width = states.shape
    block = 192 if rows % 192 == 0 else rows
    return pl.pallas_call(
        hidden_kernel,
        grid=(rows // block,),
        in_specs=[
            pl.BlockSpec((1, block, width), lambda i: (0, i, 0)),
            pl.BlockSpec((1, width), lambda i: (0, 0)),
        ],
        out_specs=pl.BlockSpec((block, width), lambda i: (i, 0)),
        out_shape=jax.ShapeDtypeStruct((rows, width), jnp.bfloat16),
        compiler_params=pltpu.CompilerParams(vmem_limit_bytes=VMEM_LIMIT),
        cost_estimate=cost(5),
        name="hidden",
    )(states, scale)


def phase(*values):
    return lax.optimization_barrier(values)


def cost(micros):
    return pl.CostEstimate(flops=int(micros * 1e3 * COST), bytes_accessed=1024, transcendentals=0)


def here():
    t = lax.axis_index("tm")
    return lax.axis_index("group"), t, lax.axis_index("tensor"), t % 2


def move(sources, place, sems):
    copies = [pltpu.make_async_copy(src, dst, sems.at[n]) for n, (src, dst) in enumerate(zip(sources, place))]
    for copy in copies:
        copy.start()
    return copies


def params():
    return pltpu.CompilerParams(vmem_limit_bytes=VMEM_LIMIT)


def first_kernel(wq, wk, wv, mine, theirs, a, b, sems):
    g, _, _, core = here()
    half = a.shape[0]
    row = pl.multiple_of(g * half, 16)
    chunks = wq.shape[1] // (2 * HD)
    waits = []
    for m, (buf, out, who) in enumerate(((a, mine, core), (b, theirs, 1 - core))):
        col = pl.multiple_of(who * (chunks * HD), HD)
        src = [w.at[pl.ds(row, half), pl.ds(col, HD)] for w in (wq, wk, wv)]
        dst = [buf.at[:, n * HD : (n + 1) * HD] for n in range(3)]
        waits.append(move(src, dst, sems.at[pl.ds(4 * m, 3)]))
    for m, (buf, out) in enumerate(((a, mine), (b, theirs))):
        for copy in waits[m]:
            copy.wait()
        pltpu.make_async_copy(buf, out, sems.at[4 * m + 3]).start()
    for m, (buf, out) in enumerate(((a, mine), (b, theirs))):
        pltpu.make_async_copy(buf, out, sems.at[4 * m + 3]).wait()


def first_packs(weights):
    half = weights[0].shape[0] // 2
    shape = (half, 3 * HD)
    return pl.pallas_call(
        first_kernel,
        in_specs=[ANY] * 3,
        out_specs=[ANY] * 2,
        out_shape=[jax.ShapeDtypeStruct(shape, jnp.bfloat16)] * 2,
        scratch_shapes=[pltpu.VMEM(shape, jnp.bfloat16)] * 2 + [pltpu.SemaphoreType.DMA((8,))],
        compiler_params=params(),
        cost_estimate=cost(1),
        name="first_packs",
    )(*weights)


def packs_kernel(wq, wk, wv, pq, pk, pv, w_out, *refs):
    chunks = wq.shape[1] // (2 * HD)
    outs, bufs, (sems,) = refs[: chunks + 1], refs[chunks + 1 : 2 * (chunks + 1)], refs[2 * (chunks + 1) :]
    g, _, z, core = here()
    half = wq.shape[0] // 2
    share = w_out.shape[1] // 2
    row = pl.multiple_of(g * half, 16)
    waits = []
    for j in range(1, chunks):
        col = pl.multiple_of(core * (chunks * HD) + j * HD, HD)
        src = [w.at[pl.ds(row, half), pl.ds(col, HD)] for w in (wq, wk, wv, pq, pk, pv)]
        dst = [
            bufs[j - 1].at[(n // 3) * half : (n // 3 + 1) * half, (n % 3) * HD : (n % 3 + 1) * HD] for n in range(6)
        ]
        waits.append(move(src, dst, sems.at[pl.ds(6 * (j - 1), 6)]))
    base = 6 * (chunks - 1)
    for k in range(2):
        at = pl.multiple_of((k ^ (z // 2)) * share, HD)
        waits.append(move([w_out.at[:, pl.ds(at, share)]], [bufs[chunks - 1 + k]], sems.at[pl.ds(base + k, 1)]))
    for n, copies in enumerate(waits):
        for copy in copies:
            copy.wait()
        pltpu.make_async_copy(bufs[n], outs[n], sems.at[base + 2 + n]).start()
    for n in range(chunks + 1):
        pltpu.make_async_copy(bufs[n], outs[n], sems.at[base + 2 + n]).wait()


def packs(own, partner, w_out):
    depth, cols = own[0].shape
    chunks = cols // (2 * HD)
    shapes = [(depth, 3 * HD)] * (chunks - 1) + [(w_out.shape[0], w_out.shape[1] // 2)] * 2
    return pl.pallas_call(
        packs_kernel,
        in_specs=[ANY] * 7,
        out_specs=[ANY] * len(shapes),
        out_shape=[jax.ShapeDtypeStruct(shape, jnp.bfloat16) for shape in shapes],
        scratch_shapes=[pltpu.VMEM(shape, jnp.bfloat16) for shape in shapes]
        + [pltpu.SemaphoreType.DMA((6 * (chunks - 1) + 2 + len(shapes),))],
        compiler_params=params(),
        cost_estimate=cost(1),
        name="packs",
    )(*own, *partner, w_out)


def near_kernel(h_own, h_par, wq, wk, wv, pq, pk, pv, out, hbuf, wbuf, obuf, hsems, wsems, osems):
    _, t, _, core = here()
    depth = wq.shape[0]
    chunks = wq.shape[1] // (2 * HD)
    wide = chunks * HD
    head = pl.multiple_of(core * wide, HD)
    spans = [slice(m * depth, (m + 1) * depth) for m in range(2)]
    at = [pl.multiple_of(owner * depth, HD) for owner in (t, t ^ 1)]

    def hidden_part(i, h):
        src = [h.at[:, pl.ds(at[m], depth)] for m in range(2)]
        return move(src, [hbuf.at[i, :, spans[m]] for m in range(2)], hsems.at[pl.ds(2 * i, 2)])

    hcopies = [hidden_part(0, h_own)]
    wcopies = []
    for n, pair in enumerate(((wq, pq), (wk, pk), (wv, pv))):
        src = [w.at[:, pl.ds(head, wide)] for w in pair]
        dst = [wbuf.at[spans[m], n * wide : (n + 1) * wide] for m in range(2)]
        wcopies.append(move(src, dst, wsems.at[pl.ds(2 * n, 2)]))
    hcopies.append(hidden_part(1, h_par))
    cols = 3 * wide
    last = []
    for i in range(2):
        for copy in hcopies[i]:
            copy.wait()
        ready = 0
        for low in range(0, cols, 256):
            tile = slice(low, min(low + 256, cols))
            while i == 0 and ready * wide < tile.stop:
                for copy in wcopies[ready]:
                    copy.wait()
                ready += 1
            obuf[i, :, tile] = jnp.dot(hbuf[i], wbuf[:, tile], preferred_element_type=jnp.float32)
        src = [obuf.at[i, :, n * wide + j * HD : n * wide + (j + 1) * HD] for j in range(chunks) for n in range(3)]
        dst = [out.at[j, i, :, n * HD : (n + 1) * HD] for j in range(chunks) for n in range(3)]
        last += move(src, dst, osems.at[pl.ds(i * 3 * chunks, 3 * chunks)])
    for copy in last:
        copy.wait()


def near(hidden, beside, weights):
    rows, _ = hidden.shape
    depth, cols = weights[0].shape
    chunks = cols // (2 * HD)
    return pl.pallas_call(
        near_kernel,
        in_specs=[ANY] * 8,
        out_specs=ANY,
        out_shape=jax.ShapeDtypeStruct((chunks, 2, rows, 3 * HD), jnp.float32),
        scratch_shapes=[
            pltpu.VMEM((2, rows, 2 * depth), jnp.bfloat16),
            pltpu.VMEM((2 * depth, 3 * HD * chunks), jnp.bfloat16),
            pltpu.VMEM((2, rows, 3 * HD * chunks), jnp.float32),
            pltpu.SemaphoreType.DMA((4,)),
            pltpu.SemaphoreType.DMA((6,)),
            pltpu.SemaphoreType.DMA((6 * chunks,)),
        ],
        compiler_params=params(),
        cost_estimate=cost(10),
        name="near",
    )(hidden, beside, *weights)


def attend_kernel(chunk, row, parts, h_own, h_par, acc, qg, kg, *refs):
    pieces, (out, hbuf, wbuf, abuf, hsems, wsems, asems) = refs[:parts], refs[parts:]
    g, t, _, core = here()
    rows = hbuf.shape[1]
    half = hbuf.shape[2] // 4
    tall = 4 * half // parts
    chunks = qg.shape[1] // (2 * HD)
    starts = [(t ^ (2 + n % 2)) * (2 * half) + (g if n < 2 else 1 - g) * half for n in range(4)]
    wcopies, hcopies, acopies = [], [[], []], []
    for part in range(2):
        some = range(part * parts // 2, (part + 1) * parts // 2)
        dst = [wbuf.at[n * tall : (n + 1) * tall, :] for n in some]
        wcopies.append(move([pieces[n] for n in some], dst, wsems.at[pl.ds(part * parts // 2, parts // 2)]))
        for i, h in enumerate((h_own, h_par)):
            src = [h.at[:, pl.ds(pl.multiple_of(starts[n], HD), half)] for n in (2 * part, 2 * part + 1)]
            dst = [hbuf.at[i, :, n * half : (n + 1) * half] for n in (2 * part, 2 * part + 1)]
            hcopies[i].append(move(src, dst, hsems.at[pl.ds(4 * i + 2 * part, 2)]))
            if part == 0:
                acopies += move([acc.at[row, i]], [abuf.at[i]], asems.at[pl.ds(i, 1)])
    head = pl.multiple_of(core * (chunks * HD) + chunk * HD, HD)

    def normed(values, gain):
        scale = lax.rsqrt(jnp.mean(values * values, axis=-1, keepdims=True) + 1e-06)
        return (values * scale * gain).astype(jnp.bfloat16)

    block = rows // 2
    for i in range(2):
        for part in range(2):
            if i == 0:
                for copy in wcopies[part]:
                    copy.wait()
            for copy in hcopies[i][part]:
                copy.wait()
            if part == 0:
                acopies[i].wait()
            span = slice(2 * part * half, 2 * (part + 1) * half)
            abuf[i] += jnp.dot(hbuf[i, :, span], wbuf[span, :], preferred_element_type=jnp.float32)
        qn = normed(abuf[i, :, :HD], qg[:, pl.ds(head, HD)])
        kn = normed(abuf[i, :, HD : 2 * HD], kg[:, pl.ds(head, HD)])
        vb = abuf[i, :, 2 * HD :].astype(jnp.bfloat16)
        for r in range(2):
            scores = lax.dot_general(
                qn[r * block : (r + 1) * block],
                kn,
                (((1,), (1,)), ((), ())),
                preferred_element_type=jnp.float32,
            )
            top = jnp.max(scores, axis=-1, keepdims=True)
            grown = jnp.exp2((scores - top) * (math.log2(math.e) / math.sqrt(HD)))
            probs = grown * (1.0 / jnp.sum(grown, axis=-1, keepdims=True))
            out[i, r * block : (r + 1) * block, :] = jnp.dot(
                probs.astype(jnp.bfloat16), vb, preferred_element_type=jnp.float32
            ).astype(jnp.bfloat16)


def attend(chunk, hidden, beside, acc, row, pieces, qg, kg):
    rows = hidden.shape[0]
    parts = len(pieces)
    depth = sum(p.shape[0] for p in pieces)
    return pl.pallas_call(
        functools.partial(attend_kernel, chunk, row, parts),
        in_specs=[ANY] * 3 + [VMEM] * 2 + [ANY] * parts,
        out_specs=VMEM,
        out_shape=jax.ShapeDtypeStruct((2, rows, HD), jnp.bfloat16),
        scratch_shapes=[
            pltpu.VMEM((2, rows, depth), jnp.bfloat16),
            pltpu.VMEM((depth, 3 * HD), jnp.bfloat16),
            pltpu.VMEM((2, rows, 3 * HD), jnp.float32),
            pltpu.SemaphoreType.DMA((8,)),
            pltpu.SemaphoreType.DMA((parts,)),
            pltpu.SemaphoreType.DMA((2,)),
        ],
        compiler_params=params(),
        cost_estimate=cost(12),
        name="attend",
    )(hidden, beside, acc, qg.reshape(1, -1), kg.reshape(1, -1), *pieces)


def bundle_kernel(*refs):
    pieces, (out, buf, sems) = refs[:4], refs[4:]
    copies = move(pieces, [buf.at[d] for d in range(4)], sems.at[pl.ds(0, 4)])
    for d, copy in enumerate(copies):
        copy.wait()
        pltpu.make_async_copy(buf.at[d], out.at[d], sems.at[4 + d]).start()
    for d in range(4):
        pltpu.make_async_copy(buf.at[d], out.at[d], sems.at[4 + d]).wait()


def bundle(*pieces):
    shape = (4, *pieces[0].shape)
    return pl.pallas_call(
        bundle_kernel,
        in_specs=[ANY] * 4,
        out_specs=ANY,
        out_shape=jax.ShapeDtypeStruct(shape, pieces[0].dtype),
        scratch_shapes=[pltpu.VMEM(shape, pieces[0].dtype), pltpu.SemaphoreType.DMA((8,))],
        compiler_params=params(),
        cost_estimate=cost(1),
        name="bundle",
    )(*pieces)


def out_kernel(chunks, top, gate_own, gate_par, *refs):
    mine, theirs, pieces = refs[:chunks], refs[chunks : 2 * chunks], refs[2 * chunks : 2 * chunks + 4]
    terms, total, att, w, asems, wsems = refs[2 * chunks + 4 :]
    devices, _, rows, _ = att.shape
    group, _, plane, core = here()
    span = slice(top, top + rows)
    waits = []
    for d in range(devices):
        pairs = []
        for j in range(chunks):
            at = pl.multiple_of(core * (chunks * HD) + j * HD, HD)
            pairs.append((mine[j].at[d, :, span, :], att.at[d, :, :, pl.ds(at, HD)]))
            at = pl.multiple_of((1 - core) * (chunks * HD) + j * HD, HD)
            for i in range(2):
                pairs.append((theirs[j].at[d, 1 - i, span, :], att.at[d, i, :, pl.ds(at, HD)]))
        waits.append([pltpu.make_async_copy(a, b, asems.at[3 * chunks * d + n]) for n, (a, b) in enumerate(pairs)])
    wcopies = []
    for d in range(devices):
        block = plane ^ d
        slot = (block // 2) ^ core
        swap = (block % 2) ^ group
        which = 2 * slot + swap
        for n, piece in enumerate(pieces):
            copy = pltpu.make_async_copy(piece, w.at[d], wsems.at[d])
            pl.when(which == n)(copy.start)
        wcopies.append(pltpu.make_async_copy(pieces[0], w.at[d], wsems.at[d]))
        for copy in waits[d]:
            copy.start()
    for d in range(devices):
        wcopies[d].wait()
        for copy in waits[d]:
            copy.wait()
        for i, gate in enumerate((gate_own, gate_par)):
            place = core if i == 0 else 1 - core
            part = (
                jnp.dot(att[d, i], w[d], preferred_element_type=jnp.float32).astype(jnp.bfloat16).astype(jnp.float32)
            )
            if d > 0:
                part = terms[place] + part
            if d == devices - 1:
                part = gate[...] * part
            terms[place] = part
    total[...] = (terms[0] + terms[1]).astype(total.dtype)


def out_projection(top, count, gate_own, gate_par, mine, theirs, pieces):
    chunks = len(mine)
    devices = mine[0].shape[0]
    deep, share = pieces[0].shape
    return pl.pallas_call(
        functools.partial(out_kernel, chunks, top),
        in_specs=[VMEM, VMEM] + [ANY] * (2 * chunks + 4),
        out_specs=[VMEM, VMEM],
        out_shape=[
            jax.ShapeDtypeStruct((2, count, share), jnp.float32),
            jax.ShapeDtypeStruct((count, share), CARRY),
        ],
        scratch_shapes=[
            pltpu.VMEM((devices, 2, count, deep), jnp.bfloat16),
            pltpu.VMEM((devices, deep, share), jnp.bfloat16),
            pltpu.SemaphoreType.DMA((devices * 3 * chunks,)),
            pltpu.SemaphoreType.DMA((devices,)),
        ],
        compiler_params=params(),
        cost_estimate=cost(12),
        name="out_projection",
    )(gate_own, gate_par, *mine, *theirs, *pieces)


def close_kernel(terms, carry, start, own, par, mine, send, squares):
    _, _, _, core = here()
    first = core == 0
    low = jnp.where(first, own[...], par[...]).astype(jnp.float32)
    high = jnp.where(first, par[...], own[...]).astype(jnp.float32)
    at_low = start[...].astype(jnp.float32) + carry[...].astype(jnp.float32)
    at_high = at_low + terms[0]
    end = at_high + terms[1]
    mine[...] = jnp.where(first, at_high, end)
    send[...] = jnp.where(first, end, at_high)
    for n, gap in enumerate((at_low - low, at_high - high)):
        part = jnp.sum(gap * gap, axis=0, keepdims=True)

        @pl.when(pl.program_id(0) == 0)
        def _(n=n, part=part):
            squares[n : n + 1, :] = part

        @pl.when(pl.program_id(0) > 0)
        def _(n=n, part=part):
            squares[n : n + 1, :] += part


def close(top, terms, carry, start, own, par):
    _, count, share = terms.shape
    block = 192 if count % 192 == 0 and top % 192 == 0 else count
    skip = top // block
    whole = pl.BlockSpec((block, share), lambda i: (skip + i, 0))
    part = pl.BlockSpec((block, share), lambda i: (i, 0))
    return pl.pallas_call(
        close_kernel,
        grid=(count // block,),
        in_specs=[pl.BlockSpec((2, block, share), lambda i: (0, i, 0)), part, whole, whole, whole],
        out_specs=[part, part, pl.BlockSpec((2, share), lambda i: (0, 0))],
        out_shape=[
            jax.ShapeDtypeStruct((count, share), jnp.float32),
            jax.ShapeDtypeStruct((count, share), jnp.float32),
            jax.ShapeDtypeStruct((2, share), jnp.float32),
        ],
        compiler_params=params(),
        cost_estimate=cost(8),
        name="close",
    )(terms, carry, start, own, par)


def join_kernel(parts, *refs):
    mine, given, (out, buf, sems) = refs[:parts], refs[parts : 2 * parts], refs[2 * parts :]
    count, share = mine[0].shape
    _, _, _, core = here()
    copies = []
    for n, piece in enumerate((*mine, *given)):
        rows = slice((n % parts) * count, (n % parts + 1) * count)
        at = pl.multiple_of((core if n < parts else 1 - core) * share, HD)
        copies.append(
            (
                pltpu.make_async_copy(piece, buf.at[n], sems.at[2 * n]),
                pltpu.make_async_copy(buf.at[n], out.at[0, rows, pl.ds(at, share)], sems.at[2 * n + 1]),
            )
        )
    for come, _ in copies:
        come.start()
    for come, go in copies:
        come.wait()
        go.start()
    for _, go in copies:
        go.wait()


def join(mine, given):
    parts = len(mine)
    count, share = mine[0].shape
    return pl.pallas_call(
        functools.partial(join_kernel, parts),
        in_specs=[ANY] * (2 * parts),
        out_specs=ANY,
        out_shape=jax.ShapeDtypeStruct((1, parts * count, 2 * share), jnp.float32),
        scratch_shapes=[
            pltpu.VMEM((2 * parts, count, share), jnp.float32),
            pltpu.SemaphoreType.DMA((4 * parts,)),
        ],
        compiler_params=params(),
        cost_estimate=cost(8),
        name="join",
    )(*mine, *given)


def fast_body(
    states, timesteps, step_sizes, mod_scale, mod_gate, w_query, w_key, w_value, query_gain, key_gain, w_out
):
    latent = states[0]
    rows, width = latent.shape
    stamp = timesteps[0].astype(jnp.float32)
    t, z = lax.axis_index("tm"), lax.axis_index("tensor")
    core, chip = t % 2, t // 2
    devices = 4
    steps = range(4)
    share = mod_gate.shape[0] // 2
    chunks = w_query.shape[1] // (2 * HD)

    def over(array, axis, flip):
        return lax.ppermute(array, axis, [(i, i ^ flip) for i in range(lax.axis_size(axis))])

    def far(array):
        return over(array, "tm", 2)

    def swap(array):
        return over(array, "group", 1)

    def partner(array):
        return over(array, "tm", 1)

    def along(array, flip):
        return over(array, "tensor", flip)

    def place(group, step, tensor):
        return (group * 4 + step) * devices + tensor

    def cross(array):
        pairs = [(a * devices + b, (a ^ 2) * devices + b) for a in steps for b in range(devices) if a // 2 == b // 2]
        return lax.ppermute(array, ("tm", "tensor"), pairs)

    def to_plane(k, piece):
        pairs = [
            (place(b % 2, a, b), place(b % 2, 2 * (a // 2) + (k ^ (b // 2)), a))
            for a in steps
            for b in range(devices)
        ]
        return lax.ppermute(piece, ("group", "tm", "tensor"), pairs)

    weights = (w_query, w_key, w_value)
    others = [partner(w) for w in weights]
    own_step = jnp.stack([stamp, step_sizes[0]])
    par_step = partner(own_step)
    p0, r0 = first_packs(weights)
    p0, r0, w_out, states = phase(p0, r0, w_out, states)

    y0 = far(p0)
    z0 = over(r0, "tm", 3)
    hidden = fast_hidden(states, make_scale(stamp, mod_scale))
    s1, s2, o0, o1 = packs(weights, others, w_out)
    y0, z0, hidden, s1, s2, o0, o1, states, own_step, par_step = phase(
        y0, z0, hidden, s1, s2, o0, o1, states, own_step, par_step
    )

    beside = partner(hidden)
    y1, x0, xz0, sent0 = far(s1), swap(y0), swap(z0), to_plane(0, o0)
    acc = near(hidden, beside, (*weights, *others))
    y1, x0, xz0, acc, beside, s2, o1, sent0, states = phase(y1, x0, xz0, acc, beside, s2, o1, sent0, states)

    x1, y2, sent1 = swap(y1), far(s2), to_plane(1, o1)
    att0 = attend(0, hidden, beside, acc, 0, (y0, z0, x0, xz0), query_gain, key_gain)
    att0, states = phase(att0, states)
    two0, one0 = along(att0, 2), along(att0, 1)
    base = z * (2 * share)
    lat_own = lax.dynamic_slice_in_dim(states[0], base + core * share, share, 1)
    lat_give = lax.dynamic_slice_in_dim(states[0], base + (1 - core) * share, share, 1)
    y2, x1, sent1, acc, lat_own, lat_give = phase(y2, x1, sent1, acc, lat_own, lat_give)

    x2, u0, three0 = swap(y2), cross(sent0), along(att0, 3)
    lat_par = partner(lat_give)
    att1 = attend(1, hidden, beside, acc, 1, (y1, x1), query_gain, key_gain)
    u0, x2, sent1, att1, two0, one0, three0, lat_own, lat_par = phase(
        u0, x2, sent1, att1, two0, one0, three0, lat_own, lat_par
    )

    home = chip == z // 2
    v0 = jnp.where(home, sent0, u0)
    xv0, u1 = swap(v0), cross(sent1)
    two1, one1, three1 = along(att1, 2), along(att1, 1), along(att1, 3)
    att2 = attend(2, hidden, beside, acc, 2, (y2, x2), query_gain, key_gain)
    u1, xv0, v0, att2, two1, one1, three1, lat_own, lat_par = phase(
        u1, xv0, v0, att2, two1, one1, three1, lat_own, lat_par
    )

    two2, one2, three2 = along(att2, 2), along(att2, 1), along(att2, 3)
    v1 = jnp.where(home, sent1, u1)
    xv1 = swap(v1)
    start_near = jnp.where(core == 0, lat_own, lat_par)
    start_far = lax.ppermute(start_near, "tm", [(0, 2), (1, 3)])
    g0 = bundle(att0, one0, two0, three0)
    g1 = bundle(att1, one1, two1, three1)
    gates = []
    for pair in (own_step, par_step):
        gate = pair[1] * make_gate(pair[0], mod_gate, width)
        gates.append(lax.dynamic_slice_in_dim(gate, core * share, share, 0).reshape(1, share))
    two2, one2, three2, v1, xv1, start_far, start_near, g0, g1, *gates = phase(
        two2, one2, three2, v1, xv1, start_far, start_near, g0, g1, *gates
    )
    gate_own, gate_par = gates

    q0, q1 = partner(g0), partner(g1)
    g2 = bundle(att2, one2, two2, three2)
    start = jnp.where(chip == 0, start_near, start_far)
    q0, q1, g2, start = phase(q0, q1, g2, start)
    q2 = partner(g2)
    pieces = [v0, xv0, v1, xv1]

    count = rows // 2

    def project(top, gate_own):
        return out_projection(top, count, gate_own, gate_par, [g0, g1, g2], [q0, q1, q2], pieces)

    def ahead(total):
        return lax.ppermute(total, "tm", [(0, 2), (1, 3)])

    terms0, total0 = project(0, gate_own)
    terms0, total0, gate_own = phase(terms0, total0, gate_own)
    carry0 = ahead(total0)
    terms1, total1 = project(count, gate_own)
    terms1, total1, carry0, start = phase(terms1, total1, carry0, start)
    carry1 = ahead(total1)
    own0, send0, squares0 = close(0, terms0, carry0, start, lat_own, lat_par)
    carry1, own0, send0, squares0, start = phase(carry1, own0, send0, squares0, start)
    given0 = partner(send0)
    own1, send1, squares1 = close(count, terms1, carry1, start, lat_own, lat_par)
    given0, own1, send1, squares = phase(given0, own1, send1, squares0 + squares1)
    given1, squares_par = partner(send1), partner(squares)
    given1, squares = phase(given1, squares + squares_par)
    sums = jnp.sum(squares, axis=1)
    next_share = join([own0, own1], [given0, given1])
    sums, next_share = phase(sums, next_share)
    sums = sums + along(sums, 1) + along(sums, 2) + along(sums, 3)
    errors = (lax.dynamic_slice_in_dim(sums, core, 1, 0) / (rows * width)).reshape(1, 1)
    return (next_share, errors)


def solution(mesh):
    placed = (
        P("tm", "group", None),
        P("tm"),
        P("tm"),
        P(),
        P("tensor"),
        P("tm", "tensor"),
        P("tm", "tensor"),
        P("tm", "tensor"),
        P("tensor"),
        P("tensor"),
        P("tensor", "tm"),
    )
    fast = mesh.shape["group"] == 2 and mesh.shape["tm"] == 4 and mesh.shape["tensor"] == 4
    return jax.shard_map(
        fast_body if fast else general_body,
        mesh=mesh,
        in_specs=placed,
        out_specs=(P("tm", "group", "tensor"), P("group", "tm")),
        check_vma=False,
    )
```

```python
import functools
import math

import jax
import jax.numpy as jnp
from jax import lax
from jax.experimental import pallas as pl
from jax.experimental.pallas import tpu as pltpu
from jax.sharding import PartitionSpec as P

HD = 128
CARRY = jnp.bfloat16
COST = 1e6
VMEM_LIMIT = 56 * 2**20
ANY = pl.BlockSpec(memory_space=pltpu.HBM)
FREE = pl.BlockSpec(memory_space=pl.ANY)
VMEM = pl.BlockSpec(memory_space=pltpu.VMEM)


def spread(block, axis, holder):
    block = jnp.where(lax.axis_index(axis) == holder, block, jnp.zeros_like(block))
    return lax.psum(block, axis)


def from_behind(array, axis, by):
    devices = lax.axis_size(axis)
    pairs = [(i, i + by) for i in range(devices) if 0 <= i + by < devices]
    return lax.ppermute(array, axis, pairs)


def head_norm(values, gain):
    rows = values.shape[0]
    count = values.shape[1] // HD
    split = values.reshape(rows, count, HD)
    normed = split * lax.rsqrt(jnp.mean(split * split, axis=-1, keepdims=True) + 1e-06)
    return (normed * gain.reshape(count, HD)).astype(jnp.bfloat16)


def make_hidden(latent, stamp, mod_scale):
    width = latent.shape[1]
    omega = jnp.exp(-math.log(10000.0) * jnp.arange(width).astype(jnp.float32) / width)
    values = latent.astype(jnp.float32)
    normed = values * lax.rsqrt(jnp.mean(values * values, axis=-1, keepdims=True) + 1e-06)
    return (normed * (1.0 + mod_scale * jnp.cos(stamp * omega))).astype(jnp.bfloat16)


def make_gate(stamp, mod_gate, width):
    share = mod_gate.shape[0]
    offset = lax.axis_index("tensor") * share
    positions = (offset + jnp.arange(share)).astype(jnp.float32)
    omega_share = jnp.exp(-math.log(10000.0) * positions / width)
    return 1.0 + mod_gate * jnp.sin(stamp * omega_share)


def general_body(
    states, timesteps, step_sizes, mod_scale, mod_gate, w_query, w_key, w_value, query_gain, key_gain, w_out
):
    latent = states[0]
    rows, width = latent.shape
    stamp = timesteps[0].astype(jnp.float32)
    hidden = make_hidden(latent, stamp, mod_scale)
    local_heads = w_query.shape[1]

    def project(weight):
        whole = lax.all_gather(weight, "tm", axis=0, tiled=True)
        return jnp.dot(hidden, whole, preferred_element_type=jnp.float32)

    count = local_heads // HD
    q_norm = head_norm(project(w_query), query_gain)
    k_norm = head_norm(project(w_key), key_gain)
    v_heads = project(w_value).astype(jnp.bfloat16).reshape(rows, count, HD)
    scores = jnp.einsum("qhd,khd->hqk", q_norm, k_norm, preferred_element_type=jnp.float32) / math.sqrt(HD)
    probs = jax.nn.softmax(scores, axis=-1).astype(jnp.bfloat16)
    attended = jnp.einsum("hqk,khd->qhd", probs, v_heads, preferred_element_type=jnp.float32)
    attended = attended.astype(jnp.bfloat16).reshape(rows, local_heads)
    share = mod_gate.shape[0]
    offset = lax.axis_index("tensor") * share
    partial_out = jnp.dot(
        attended,
        lax.all_gather(w_out, "tm", axis=1, tiled=True),
        preferred_element_type=jnp.float32,
    )
    projected = lax.psum_scatter(
        partial_out.astype(jnp.bfloat16), "tensor", scatter_dimension=1, tiled=True
    ).astype(jnp.float32)
    term = step_sizes[0] * make_gate(stamp, mod_gate, width) * projected
    own_slice = lax.dynamic_slice_in_dim(latent, offset, share, 1)
    own_start = own_slice.astype(jnp.float32)
    base_state = spread(own_slice, "tm", 0).astype(jnp.float32)
    running = term
    for level in range((lax.axis_size("tm") - 1).bit_length()):
        running = running + from_behind(running, "tm", 1 << level)
    before = running - term
    predicted = base_state + before
    next_share = predicted + term
    gap = predicted - own_start
    squared = lax.psum(jnp.sum(gap * gap), "tensor")
    errors = (squared / (rows * width)).reshape(1, 1)
    return (next_share[None], errors)


def after(value, *others):
    return lax.optimization_barrier((value, *others))[0]


def hidden_kernel(latent, scale, out):
    values = latent[0].astype(jnp.float32)
    normed = values * lax.rsqrt(jnp.mean(values * values, axis=-1, keepdims=True) + 1e-06)
    out[...] = (normed * scale[...]).astype(jnp.bfloat16)


def make_scale(stamp, mod_scale):
    width = mod_scale.shape[0]
    omega = jnp.exp(-math.log(10000.0) * jnp.arange(width).astype(jnp.float32) / width)
    return (1.0 + mod_scale * jnp.cos(stamp * omega)).reshape(1, width)


def fast_hidden(states, scale):
    _, rows, width = states.shape
    block = 192 if rows % 192 == 0 else rows
    return pl.pallas_call(
        hidden_kernel,
        grid=(rows // block,),
        in_specs=[
            pl.BlockSpec((1, block, width), lambda i: (0, i, 0)),
            pl.BlockSpec((1, width), lambda i: (0, 0)),
        ],
        out_specs=pl.BlockSpec((block, width), lambda i: (i, 0)),
        out_shape=jax.ShapeDtypeStruct((rows, width), jnp.bfloat16),
        compiler_params=pltpu.CompilerParams(vmem_limit_bytes=VMEM_LIMIT),
        cost_estimate=cost(5),
        name="hidden",
    )(states, scale)


def phase(*values):
    return lax.optimization_barrier(values)


def cost(micros):
    return pl.CostEstimate(flops=int(micros * 1e3 * COST), bytes_accessed=1024, transcendentals=0)


def here():
    t = lax.axis_index("tm")
    return lax.axis_index("group"), t, lax.axis_index("tensor"), t % 2


def move(sources, place, sems):
    copies = [pltpu.make_async_copy(src, dst, sems.at[n]) for n, (src, dst) in enumerate(zip(sources, place))]
    for copy in copies:
        copy.start()
    return copies


def params():
    return pltpu.CompilerParams(vmem_limit_bytes=VMEM_LIMIT)


def first_kernel(wq, wk, wv, mine, theirs, a, b, sems):
    g, _, _, core = here()
    half = a.shape[0]
    row = pl.multiple_of(g * half, 16)
    chunks = wq.shape[1] // (2 * HD)
    waits = []
    for m, (buf, out, who) in enumerate(((a, mine, core), (b, theirs, 1 - core))):
        col = pl.multiple_of(who * (chunks * HD), HD)
        src = [w.at[pl.ds(row, half), pl.ds(col, HD)] for w in (wq, wk, wv)]
        dst = [buf.at[:, n * HD : (n + 1) * HD] for n in range(3)]
        waits.append(move(src, dst, sems.at[pl.ds(4 * m, 3)]))
    for m, (buf, out) in enumerate(((a, mine), (b, theirs))):
        for copy in waits[m]:
            copy.wait()
        pltpu.make_async_copy(buf, out, sems.at[4 * m + 3]).start()
    for m, (buf, out) in enumerate(((a, mine), (b, theirs))):
        pltpu.make_async_copy(buf, out, sems.at[4 * m + 3]).wait()


def first_packs(weights):
    half = weights[0].shape[0] // 2
    shape = (half, 3 * HD)
    return pl.pallas_call(
        first_kernel,
        in_specs=[ANY] * 3,
        out_specs=[ANY] * 2,
        out_shape=[jax.ShapeDtypeStruct(shape, jnp.bfloat16)] * 2,
        scratch_shapes=[pltpu.VMEM(shape, jnp.bfloat16)] * 2 + [pltpu.SemaphoreType.DMA((8,))],
        compiler_params=params(),
        cost_estimate=cost(1),
        name="first_packs",
    )(*weights)


def packs_kernel(wq, wk, wv, pq, pk, pv, w_out, *refs):
    chunks = wq.shape[1] // (2 * HD)
    outs, bufs, (sems,) = refs[: chunks + 1], refs[chunks + 1 : 2 * (chunks + 1)], refs[2 * (chunks + 1) :]
    g, _, z, core = here()
    half = wq.shape[0] // 2
    share = w_out.shape[1] // 2
    row = pl.multiple_of(g * half, 16)
    waits = []
    for j in range(1, chunks):
        col = pl.multiple_of(core * (chunks * HD) + j * HD, HD)
        src = [w.at[pl.ds(row, half), pl.ds(col, HD)] for w in (wq, wk, wv, pq, pk, pv)]
        dst = [
            bufs[j - 1].at[(n // 3) * half : (n // 3 + 1) * half, (n % 3) * HD : (n % 3 + 1) * HD] for n in range(6)
        ]
        waits.append(move(src, dst, sems.at[pl.ds(6 * (j - 1), 6)]))
    base = 6 * (chunks - 1)
    for k in range(2):
        at = pl.multiple_of((k ^ (z // 2)) * share, HD)
        waits.append(move([w_out.at[:, pl.ds(at, share)]], [bufs[chunks - 1 + k]], sems.at[pl.ds(base + k, 1)]))
    for n, copies in enumerate(waits):
        for copy in copies:
            copy.wait()
        pltpu.make_async_copy(bufs[n], outs[n], sems.at[base + 2 + n]).start()
    for n in range(chunks + 1):
        pltpu.make_async_copy(bufs[n], outs[n], sems.at[base + 2 + n]).wait()


def packs(own, partner, w_out):
    depth, cols = own[0].shape
    chunks = cols // (2 * HD)
    shapes = [(depth, 3 * HD)] * (chunks - 1) + [(w_out.shape[0], w_out.shape[1] // 2)] * 2
    return pl.pallas_call(
        packs_kernel,
        in_specs=[ANY] * 7,
        out_specs=[ANY] * len(shapes),
        out_shape=[jax.ShapeDtypeStruct(shape, jnp.bfloat16) for shape in shapes],
        scratch_shapes=[pltpu.VMEM(shape, jnp.bfloat16) for shape in shapes]
        + [pltpu.SemaphoreType.DMA((6 * (chunks - 1) + 2 + len(shapes),))],
        compiler_params=params(),
        cost_estimate=cost(1),
        name="packs",
    )(*own, *partner, w_out)


def near_kernel(h_own, h_par, wq, wk, wv, pq, pk, pv, out, hbuf, wbuf, obuf, hsems, wsems, osems):
    _, t, _, core = here()
    depth = wq.shape[0]
    chunks = wq.shape[1] // (2 * HD)
    wide = chunks * HD
    head = pl.multiple_of(core * wide, HD)
    spans = [slice(m * depth, (m + 1) * depth) for m in range(2)]
    at = [pl.multiple_of(owner * depth, HD) for owner in (t, t ^ 1)]

    def hidden_part(i, h):
        src = [h.at[:, pl.ds(at[m], depth)] for m in range(2)]
        return move(src, [hbuf.at[i, :, spans[m]] for m in range(2)], hsems.at[pl.ds(2 * i, 2)])

    hcopies = [hidden_part(0, h_own)]
    wcopies = []
    for n, pair in enumerate(((wq, pq), (wk, pk), (wv, pv))):
        src = [w.at[:, pl.ds(head, wide)] for w in pair]
        dst = [wbuf.at[spans[m], n * wide : (n + 1) * wide] for m in range(2)]
        wcopies.append(move(src, dst, wsems.at[pl.ds(2 * n, 2)]))
    hcopies.append(hidden_part(1, h_par))
    cols = 3 * wide
    last = []
    for i in range(2):
        for copy in hcopies[i]:
            copy.wait()
        ready = 0
        for low in range(0, cols, 256):
            tile = slice(low, min(low + 256, cols))
            while i == 0 and ready * wide < tile.stop:
                for copy in wcopies[ready]:
                    copy.wait()
                ready += 1
            obuf[i, :, tile] = jnp.dot(hbuf[i], wbuf[:, tile], preferred_element_type=jnp.float32)
        src = [obuf.at[i, :, n * wide + j * HD : n * wide + (j + 1) * HD] for j in range(chunks) for n in range(3)]
        dst = [out.at[j, i, :, n * HD : (n + 1) * HD] for j in range(chunks) for n in range(3)]
        last += move(src, dst, osems.at[pl.ds(i * 3 * chunks, 3 * chunks)])
    for copy in last:
        copy.wait()


def near(hidden, beside, weights):
    rows, _ = hidden.shape
    depth, cols = weights[0].shape
    chunks = cols // (2 * HD)
    return pl.pallas_call(
        near_kernel,
        in_specs=[ANY] * 8,
        out_specs=ANY,
        out_shape=jax.ShapeDtypeStruct((chunks, 2, rows, 3 * HD), jnp.float32),
        scratch_shapes=[
            pltpu.VMEM((2, rows, 2 * depth), jnp.bfloat16),
            pltpu.VMEM((2 * depth, 3 * HD * chunks), jnp.bfloat16),
            pltpu.VMEM((2, rows, 3 * HD * chunks), jnp.float32),
            pltpu.SemaphoreType.DMA((4,)),
            pltpu.SemaphoreType.DMA((6,)),
            pltpu.SemaphoreType.DMA((6 * chunks,)),
        ],
        compiler_params=params(),
        cost_estimate=cost(10),
        name="near",
    )(hidden, beside, *weights)


def attend_kernel(chunk, row, parts, h_own, h_par, acc, qg, kg, *refs):
    pieces, (out, hbuf, wbuf, abuf, hsems, wsems, asems) = refs[:parts], refs[parts:]
    g, t, _, core = here()
    rows = hbuf.shape[1]
    half = hbuf.shape[2] // 4
    tall = 4 * half // parts
    chunks = qg.shape[1] // (2 * HD)
    starts = [(t ^ (2 + n % 2)) * (2 * half) + (g if n < 2 else 1 - g) * half for n in range(4)]
    wcopies, hcopies, acopies = [], [[], []], []
    for part in range(2):
        some = range(part * parts // 2, (part + 1) * parts // 2)
        dst = [wbuf.at[n * tall : (n + 1) * tall, :] for n in some]
        wcopies.append(move([pieces[n] for n in some], dst, wsems.at[pl.ds(part * parts // 2, parts // 2)]))
        for i, h in enumerate((h_own, h_par)):
            src = [h.at[:, pl.ds(pl.multiple_of(starts[n], HD), half)] for n in (2 * part, 2 * part + 1)]
            dst = [hbuf.at[i, :, n * half : (n + 1) * half] for n in (2 * part, 2 * part + 1)]
            hcopies[i].append(move(src, dst, hsems.at[pl.ds(4 * i + 2 * part, 2)]))
            if part == 0:
                acopies += move([acc.at[row, i]], [abuf.at[i]], asems.at[pl.ds(i, 1)])
    head = pl.multiple_of(core * (chunks * HD) + chunk * HD, HD)

    def normed(values, gain):
        scale = lax.rsqrt(jnp.mean(values * values, axis=-1, keepdims=True) + 1e-06)
        return (values * scale * gain).astype(jnp.bfloat16)

    block = rows // 2
    for i in range(2):
        for part in range(2):
            if i == 0:
                for copy in wcopies[part]:
                    copy.wait()
            for copy in hcopies[i][part]:
                copy.wait()
            if part == 0:
                acopies[i].wait()
            span = slice(2 * part * half, 2 * (part + 1) * half)
            abuf[i] += jnp.dot(hbuf[i, :, span], wbuf[span, :], preferred_element_type=jnp.float32)
        qn = normed(abuf[i, :, :HD], qg[:, pl.ds(head, HD)])
        kn = normed(abuf[i, :, HD : 2 * HD], kg[:, pl.ds(head, HD)])
        vb = abuf[i, :, 2 * HD :].astype(jnp.bfloat16)
        for r in range(2):
            scores = lax.dot_general(
                qn[r * block : (r + 1) * block],
                kn,
                (((1,), (1,)), ((), ())),
                preferred_element_type=jnp.float32,
            )
            top = jnp.max(scores, axis=-1, keepdims=True)
            grown = jnp.exp2((scores - top) * (math.log2(math.e) / math.sqrt(HD)))
            probs = grown * (1.0 / jnp.sum(grown, axis=-1, keepdims=True))
            out[i, r * block : (r + 1) * block, :] = jnp.dot(
                probs.astype(jnp.bfloat16), vb, preferred_element_type=jnp.float32
            ).astype(jnp.bfloat16)


def attend(chunk, hidden, beside, acc, row, pieces, qg, kg):
    rows = hidden.shape[0]
    parts = len(pieces)
    depth = sum(p.shape[0] for p in pieces)
    return pl.pallas_call(
        functools.partial(attend_kernel, chunk, row, parts),
        in_specs=[ANY] * 3 + [VMEM] * 2 + [ANY] * parts,
        out_specs=VMEM,
        out_shape=jax.ShapeDtypeStruct((2, rows, HD), jnp.bfloat16),
        scratch_shapes=[
            pltpu.VMEM((2, rows, depth), jnp.bfloat16),
            pltpu.VMEM((depth, 3 * HD), jnp.bfloat16),
            pltpu.VMEM((2, rows, 3 * HD), jnp.float32),
            pltpu.SemaphoreType.DMA((8,)),
            pltpu.SemaphoreType.DMA((parts,)),
            pltpu.SemaphoreType.DMA((2,)),
        ],
        compiler_params=params(),
        cost_estimate=cost(12),
        name="attend",
    )(hidden, beside, acc, qg.reshape(1, -1), kg.reshape(1, -1), *pieces)


def bundle_kernel(count, *refs):
    pieces, (out, buf, sems) = refs[:count], refs[count:]
    copies = move(pieces[:3], [buf.at[d] for d in range(3)], sems.at[pl.ds(0, 3)])
    copies.append(pltpu.make_async_copy(pieces[3], buf.at[3], sems.at[3]))
    if count == 4:
        copies[3].start()
    else:
        _, _, z, _ = here()
        inner = jnp.logical_or(z == 1, z == 2)
        pl.when(inner)(copies[3].start)
        pl.when(jnp.logical_not(inner))(pltpu.make_async_copy(pieces[4], buf.at[3], sems.at[3]).start)
    for d, copy in enumerate(copies):
        copy.wait()
        pltpu.make_async_copy(buf.at[d], out.at[d], sems.at[4 + d]).start()
    for d in range(4):
        pltpu.make_async_copy(buf.at[d], out.at[d], sems.at[4 + d]).wait()


def bundle(*pieces):
    shape = (4, *pieces[0].shape)
    return pl.pallas_call(
        functools.partial(bundle_kernel, len(pieces)),
        in_specs=[ANY] * len(pieces),
        out_specs=ANY,
        out_shape=jax.ShapeDtypeStruct(shape, pieces[0].dtype),
        scratch_shapes=[pltpu.VMEM(shape, pieces[0].dtype), pltpu.SemaphoreType.DMA((8,))],
        compiler_params=params(),
        cost_estimate=cost(1),
        name="bundle",
    )(*pieces)


def out_kernel(chunks, top, gate_own, gate_par, *refs):
    mine, theirs, refs = refs[: chunks - 1], refs[chunks - 1 : 2 * chunks - 2], refs[2 * chunks - 2 :]
    last_mine, last_theirs, pieces = refs[:4], refs[4:8], refs[8:12]
    terms, total, att, w, asems, wsems = refs[12:]
    devices, _, rows, _ = att.shape
    group, _, plane, core = here()
    span = slice(top, top + rows)
    waits = []
    for d in range(devices):
        pairs = []
        for j in range(chunks):
            got, given = (mine[j].at[d], theirs[j].at[d]) if j < chunks - 1 else (last_mine[d], last_theirs[d])
            at = pl.multiple_of(core * (chunks * HD) + j * HD, HD)
            pairs.append((got.at[:, span, :], att.at[d, :, :, pl.ds(at, HD)]))
            at = pl.multiple_of((1 - core) * (chunks * HD) + j * HD, HD)
            for i in range(2):
                pairs.append((given.at[1 - i, span, :], att.at[d, i, :, pl.ds(at, HD)]))
        waits.append([pltpu.make_async_copy(a, b, asems.at[3 * chunks * d + n]) for n, (a, b) in enumerate(pairs)])
    wcopies = []
    for d in range(devices):
        block = plane ^ d
        slot = (block // 2) ^ core
        swap = (block % 2) ^ group
        which = 2 * slot + swap
        for n, piece in enumerate(pieces):
            copy = pltpu.make_async_copy(piece, w.at[d], wsems.at[d])
            pl.when(which == n)(copy.start)
        wcopies.append(pltpu.make_async_copy(pieces[0], w.at[d], wsems.at[d]))
        for copy in waits[d]:
            copy.start()
    for d in range(devices):
        wcopies[d].wait()
        for copy in waits[d]:
            copy.wait()
        for i, gate in enumerate((gate_own, gate_par)):
            place = core if i == 0 else 1 - core
            part = (
                jnp.dot(att[d, i], w[d], preferred_element_type=jnp.float32).astype(jnp.bfloat16).astype(jnp.float32)
            )
            if d > 0:
                part = terms[place] + part
            if d == devices - 1:
                part = gate[...] * part
            terms[place] = part
    total[...] = (terms[0] + terms[1]).astype(total.dtype)


def out_projection(top, count, gate_own, gate_par, mine, theirs, last_mine, last_theirs, pieces):
    chunks = len(mine) + 1
    devices = mine[0].shape[0]
    deep, share = pieces[0].shape
    return pl.pallas_call(
        functools.partial(out_kernel, chunks, top),
        in_specs=[VMEM, VMEM] + [FREE] * (2 * chunks + 10),
        out_specs=[VMEM, VMEM],
        out_shape=[
            jax.ShapeDtypeStruct((2, count, share), jnp.float32),
            jax.ShapeDtypeStruct((count, share), CARRY),
        ],
        scratch_shapes=[
            pltpu.VMEM((devices, 2, count, deep), jnp.bfloat16),
            pltpu.VMEM((devices, deep, share), jnp.bfloat16),
            pltpu.SemaphoreType.DMA((devices * 3 * chunks,)),
            pltpu.SemaphoreType.DMA((devices,)),
        ],
        compiler_params=params(),
        cost_estimate=cost(12),
        name="out_projection",
    )(gate_own, gate_par, *mine, *theirs, *last_mine, *last_theirs, *pieces)


def close_kernel(terms, carry, far, own, par, mine, send, squares):
    _, t, _, core = here()
    first = core == 0
    low = jnp.where(first, own[...], par[...]).astype(jnp.float32)
    high = jnp.where(first, par[...], own[...]).astype(jnp.float32)
    at_low = jnp.where(t < 2, low, far[...].astype(jnp.float32)) + carry[...].astype(jnp.float32)
    at_high = at_low + terms[0]
    end = at_high + terms[1]
    mine[...] = jnp.where(first, at_high, end)
    send[...] = jnp.where(first, end, at_high)
    for n, gap in enumerate((at_low - low, at_high - high)):
        part = jnp.sum(gap * gap, axis=0, keepdims=True)

        @pl.when(pl.program_id(0) == 0)
        def _(n=n, part=part):
            squares[n : n + 1, :] = part

        @pl.when(pl.program_id(0) > 0)
        def _(n=n, part=part):
            squares[n : n + 1, :] += part


def close(top, terms, carry, far, own, par):
    _, count, share = terms.shape
    block = 192 if count % 192 == 0 and top % 192 == 0 else count
    skip = top // block
    whole = pl.BlockSpec((block, share), lambda i: (skip + i, 0))
    part = pl.BlockSpec((block, share), lambda i: (i, 0))
    return pl.pallas_call(
        close_kernel,
        grid=(count // block,),
        in_specs=[pl.BlockSpec((2, block, share), lambda i: (0, i, 0)), part, whole, whole, whole],
        out_specs=[part, part, pl.BlockSpec((2, share), lambda i: (0, 0))],
        out_shape=[
            jax.ShapeDtypeStruct((count, share), jnp.float32),
            jax.ShapeDtypeStruct((count, share), jnp.float32),
            jax.ShapeDtypeStruct((2, share), jnp.float32),
        ],
        compiler_params=params(),
        cost_estimate=cost(8),
        name="close",
    )(terms, carry, far, own, par)


def join_kernel(parts, *refs):
    mine, given, (out, buf, sems) = refs[:parts], refs[parts : 2 * parts], refs[2 * parts :]
    count, share = mine[0].shape
    _, _, _, core = here()
    copies = []
    for n, piece in enumerate((*mine, *given)):
        rows = slice((n % parts) * count, (n % parts + 1) * count)
        at = pl.multiple_of((core if n < parts else 1 - core) * share, HD)
        copies.append(
            (
                pltpu.make_async_copy(piece, buf.at[n], sems.at[2 * n]),
                pltpu.make_async_copy(buf.at[n], out.at[0, rows, pl.ds(at, share)], sems.at[2 * n + 1]),
            )
        )
    for come, _ in copies:
        come.start()
    for come, go in copies:
        come.wait()
        go.start()
    for _, go in copies:
        go.wait()


def join(mine, given):
    parts = len(mine)
    count, share = mine[0].shape
    return pl.pallas_call(
        functools.partial(join_kernel, parts),
        in_specs=[ANY] * (2 * parts),
        out_specs=ANY,
        out_shape=jax.ShapeDtypeStruct((1, parts * count, 2 * share), jnp.float32),
        scratch_shapes=[
            pltpu.VMEM((2 * parts, count, share), jnp.float32),
            pltpu.SemaphoreType.DMA((4 * parts,)),
        ],
        compiler_params=params(),
        cost_estimate=cost(8),
        name="join",
    )(*mine, *given)


def fast_body(
    states, timesteps, step_sizes, mod_scale, mod_gate, w_query, w_key, w_value, query_gain, key_gain, w_out
):
    latent = states[0]
    rows, width = latent.shape
    stamp = timesteps[0].astype(jnp.float32)
    t, z = lax.axis_index("tm"), lax.axis_index("tensor")
    core, chip = t % 2, t // 2
    devices = 4
    steps = range(4)
    share = mod_gate.shape[0] // 2
    chunks = w_query.shape[1] // (2 * HD)

    def over(array, axis, flip):
        return lax.ppermute(array, axis, [(i, i ^ flip) for i in range(lax.axis_size(axis))])

    def far(array):
        return over(array, "tm", 2)

    def swap(array):
        return over(array, "group", 1)

    def partner(array):
        return over(array, "tm", 1)

    def along(array, flip):
        return over(array, "tensor", flip)

    def middle(array):
        return lax.ppermute(array, "tensor", [(1, 2), (2, 1)])

    def outward(array):
        return lax.ppermute(array, "tensor", [(1, 0), (2, 3)])

    def place(group, step, tensor):
        return (group * 4 + step) * devices + tensor

    def cross(array):
        pairs = [(a * devices + b, (a ^ 2) * devices + b) for a in steps for b in range(devices) if a // 2 == b // 2]
        return lax.ppermute(array, ("tm", "tensor"), pairs)

    def to_plane(k, piece):
        pairs = [
            (place(b % 2, a, b), place(b % 2, 2 * (a // 2) + (k ^ (b // 2)), a))
            for a in steps
            for b in range(devices)
        ]
        return lax.ppermute(piece, ("group", "tm", "tensor"), pairs)

    weights = (w_query, w_key, w_value)
    others = [partner(w) for w in weights]
    own_step = jnp.stack([stamp, step_sizes[0]])
    par_step = partner(own_step)
    p0, r0 = first_packs(weights)
    p0, r0, w_out, states = phase(p0, r0, w_out, states)

    y0 = far(p0)
    z0 = over(r0, "tm", 3)
    base = z * (2 * share)
    lat_own = lax.dynamic_slice_in_dim(states[0], base + core * share, share, 1)
    lat_give = lax.dynamic_slice_in_dim(states[0], base + (1 - core) * share, share, 1)
    lat_par = partner(lat_give)
    hidden = fast_hidden(states, make_scale(stamp, mod_scale))
    s1, s2, o0, o1 = packs(weights, others, w_out)
    y0, z0, hidden, s1, s2, o0, o1, lat_own, lat_par, own_step, par_step = phase(
        y0, z0, hidden, s1, s2, o0, o1, lat_own, lat_par, own_step, par_step
    )

    beside = partner(hidden)
    y1, x0, xz0, sent0, sent1 = far(s1), swap(y0), swap(z0), to_plane(0, o0), to_plane(1, o1)
    acc = near(hidden, beside, (*weights, *others))
    y1, x0, xz0, acc, beside, s2, sent0 = phase(y1, x0, xz0, acc, beside, s2, sent0)

    x1, y2 = swap(y1), far(s2)
    att0 = attend(0, hidden, beside, acc, 0, (y0, z0, x0, xz0), query_gain, key_gain)
    att0, own_step, par_step, sent1 = phase(att0, own_step, par_step, sent1)
    two0, one0 = along(att0, 2), along(att0, 1)
    gates = []
    for pair in (own_step, par_step):
        gate = pair[1] * make_gate(pair[0], mod_gate, width)
        gates.append(lax.dynamic_slice_in_dim(gate, core * share, share, 0).reshape(1, share))
    y2, x1, acc, *gates = phase(y2, x1, acc, *gates)

    x2, u0, inner0 = swap(y2), cross(sent0), middle(att0)
    att1 = attend(1, hidden, beside, acc, 1, (y1, x1), query_gain, key_gain)
    att1, two0, v0 = phase(att1, two0, sent0)
    outer0, two1 = outward(two0), along(att1, 2)
    u0, x2, one0, inner0, outer0, v0 = phase(u0, x2, one0, inner0, outer0, v0)

    home = chip == z // 2
    v0 = jnp.where(home, v0, u0)
    xv0, u1 = swap(v0), cross(sent1)
    one1, inner1 = along(att1, 1), middle(att1)
    att2 = attend(2, hidden, beside, acc, 2, (y2, x2), query_gain, key_gain)
    two1, att2 = phase(two1, att2)
    outer1, two2 = outward(two1), along(att2, 2)
    g0 = bundle(att0, one0, two0, inner0, outer0)
    u1, xv0, v0, one1, inner1, outer1, g0, lat_own, lat_par, *gates = phase(
        u1, xv0, v0, one1, inner1, outer1, g0, lat_own, lat_par, *gates
    )
    gate_own, gate_par = gates

    one2, inner2 = along(att2, 1), middle(att2)
    v1 = jnp.where(home, sent1, u1)
    xv1 = swap(v1)
    start_far = lax.ppermute(jnp.where(core == 0, lat_own, lat_par), "tm", [(0, 2), (1, 3)])
    g1 = bundle(att1, one1, two1, inner1, outer1)
    two2, one2, inner2, v1, xv1, g1, start_far = phase(two2, one2, inner2, v1, xv1, g1, start_far)
    outer2 = outward(two2)
    q0, q1, b0, b1, b2 = partner(g0), partner(g1), partner(att2), partner(one2), partner(two2)
    outer2, inner2, q0, q1, b0, b1, b2 = phase(outer2, inner2, q0, q1, b0, b1, b2)

    three2 = jnp.where(jnp.logical_or(z == 1, z == 2), inner2, outer2)
    b3 = partner(three2)
    pieces = [v0, xv0, v1, xv1]

    count = rows // 2

    def project(top, gate_own):
        mine, theirs = [att2, one2, two2, three2], [b0, b1, b2, b3]
        return out_projection(top, count, gate_own, gate_par, [g0, g1], [q0, q1], mine, theirs, pieces)

    def ahead(total):
        return lax.ppermute(total, "tm", [(0, 2), (1, 3)])

    terms0, total0 = project(0, gate_own)
    terms0, total0, gate_own = phase(terms0, total0, gate_own)
    carry0 = ahead(total0)
    terms1, total1 = project(count, gate_own)
    terms1, total1, carry0 = phase(terms1, total1, carry0)
    carry1 = ahead(total1)
    own0, send0, squares0 = close(0, terms0, carry0, start_far, lat_own, lat_par)
    carry1, own0, send0, squares0 = phase(carry1, own0, send0, squares0)
    given0 = partner(send0)
    own1, send1, squares1 = close(count, terms1, carry1, start_far, lat_own, lat_par)
    given0, own1, send1, squares = phase(given0, own1, send1, squares0 + squares1)
    given1, squares_par = partner(send1), partner(squares)
    given1, squares = phase(given1, squares + squares_par)
    sums = jnp.sum(squares, axis=1)
    sums = sums + along(sums, 1) + along(sums, 2) + along(sums, 3)
    next_share = join([own0, own1], [given0, given1])
    errors = (lax.dynamic_slice_in_dim(sums, core, 1, 0) / (rows * width)).reshape(1, 1)
    return (next_share, errors)


def solution(mesh):
    placed = (
        P("tm", "group", None),
        P("tm"),
        P("tm"),
        P(),
        P("tensor"),
        P("tm", "tensor"),
        P("tm", "tensor"),
        P("tm", "tensor"),
        P("tensor"),
        P("tensor"),
        P("tensor", "tm"),
    )
    fast = mesh.shape["group"] == 2 and mesh.shape["tm"] == 4 and mesh.shape["tensor"] == 4
    return jax.shard_map(
        fast_body if fast else general_body,
        mesh=mesh,
        in_specs=placed,
        out_specs=(P("tm", "group", "tensor"), P("group", "tm")),
        check_vma=False,
    )
```

```python
import functools
import math

import jax
import jax.numpy as jnp
from jax import lax
from jax.experimental import pallas as pl
from jax.experimental.pallas import tpu as pltpu
from jax.sharding import PartitionSpec as P

HD = 128
CARRY = jnp.bfloat16
COST = 1e6
VMEM_LIMIT = 56 * 2**20
ANY = pl.BlockSpec(memory_space=pltpu.HBM)
FREE = pl.BlockSpec(memory_space=pl.ANY)
VMEM = pl.BlockSpec(memory_space=pltpu.VMEM)


def spread(block, axis, holder):
    block = jnp.where(lax.axis_index(axis) == holder, block, jnp.zeros_like(block))
    return lax.psum(block, axis)


def from_behind(array, axis, by):
    devices = lax.axis_size(axis)
    pairs = [(i, i + by) for i in range(devices) if 0 <= i + by < devices]
    return lax.ppermute(array, axis, pairs)


def head_norm(values, gain):
    rows = values.shape[0]
    count = values.shape[1] // HD
    split = values.reshape(rows, count, HD)
    normed = split * lax.rsqrt(jnp.mean(split * split, axis=-1, keepdims=True) + 1e-06)
    return (normed * gain.reshape(count, HD)).astype(jnp.bfloat16)


def make_hidden(latent, stamp, mod_scale):
    width = latent.shape[1]
    omega = jnp.exp(-math.log(10000.0) * jnp.arange(width).astype(jnp.float32) / width)
    values = latent.astype(jnp.float32)
    normed = values * lax.rsqrt(jnp.mean(values * values, axis=-1, keepdims=True) + 1e-06)
    return (normed * (1.0 + mod_scale * jnp.cos(stamp * omega))).astype(jnp.bfloat16)


def make_gate(stamp, mod_gate, width):
    share = mod_gate.shape[0]
    offset = lax.axis_index("tensor") * share
    positions = (offset + jnp.arange(share)).astype(jnp.float32)
    omega_share = jnp.exp(-math.log(10000.0) * positions / width)
    return 1.0 + mod_gate * jnp.sin(stamp * omega_share)


def general_body(
    states, timesteps, step_sizes, mod_scale, mod_gate, w_query, w_key, w_value, query_gain, key_gain, w_out
):
    latent = states[0]
    rows, width = latent.shape
    stamp = timesteps[0].astype(jnp.float32)
    hidden = make_hidden(latent, stamp, mod_scale)
    local_heads = w_query.shape[1]

    def project(weight):
        whole = lax.all_gather(weight, "tm", axis=0, tiled=True)
        return jnp.dot(hidden, whole, preferred_element_type=jnp.float32)

    count = local_heads // HD
    q_norm = head_norm(project(w_query), query_gain)
    k_norm = head_norm(project(w_key), key_gain)
    v_heads = project(w_value).astype(jnp.bfloat16).reshape(rows, count, HD)
    scores = jnp.einsum("qhd,khd->hqk", q_norm, k_norm, preferred_element_type=jnp.float32) / math.sqrt(HD)
    probs = jax.nn.softmax(scores, axis=-1).astype(jnp.bfloat16)
    attended = jnp.einsum("hqk,khd->qhd", probs, v_heads, preferred_element_type=jnp.float32)
    attended = attended.astype(jnp.bfloat16).reshape(rows, local_heads)
    share = mod_gate.shape[0]
    offset = lax.axis_index("tensor") * share
    partial_out = jnp.dot(
        attended,
        lax.all_gather(w_out, "tm", axis=1, tiled=True),
        preferred_element_type=jnp.float32,
    )
    projected = lax.psum_scatter(
        partial_out.astype(jnp.bfloat16), "tensor", scatter_dimension=1, tiled=True
    ).astype(jnp.float32)
    term = step_sizes[0] * make_gate(stamp, mod_gate, width) * projected
    own_slice = lax.dynamic_slice_in_dim(latent, offset, share, 1)
    own_start = own_slice.astype(jnp.float32)
    base_state = spread(own_slice, "tm", 0).astype(jnp.float32)
    running = term
    for level in range((lax.axis_size("tm") - 1).bit_length()):
        running = running + from_behind(running, "tm", 1 << level)
    before = running - term
    predicted = base_state + before
    next_share = predicted + term
    gap = predicted - own_start
    squared = lax.psum(jnp.sum(gap * gap), "tensor")
    errors = (squared / (rows * width)).reshape(1, 1)
    return (next_share[None], errors)


def after(value, *others):
    return lax.optimization_barrier((value, *others))[0]


def hidden_kernel(latent, scale, out):
    values = latent[0].astype(jnp.float32)
    normed = values * lax.rsqrt(jnp.mean(values * values, axis=-1, keepdims=True) + 1e-06)
    out[...] = (normed * scale[...]).astype(jnp.bfloat16)


def make_scale(stamp, mod_scale):
    width = mod_scale.shape[0]
    omega = jnp.exp(-math.log(10000.0) * jnp.arange(width).astype(jnp.float32) / width)
    return (1.0 + mod_scale * jnp.cos(stamp * omega)).reshape(1, width)


def fast_hidden(states, scale):
    _, rows, width = states.shape
    block = 192 if rows % 192 == 0 else rows
    return pl.pallas_call(
        hidden_kernel,
        grid=(rows // block,),
        in_specs=[
            pl.BlockSpec((1, block, width), lambda i: (0, i, 0)),
            pl.BlockSpec((1, width), lambda i: (0, 0)),
        ],
        out_specs=pl.BlockSpec((block, width), lambda i: (i, 0)),
        out_shape=jax.ShapeDtypeStruct((rows, width), jnp.bfloat16),
        compiler_params=pltpu.CompilerParams(vmem_limit_bytes=VMEM_LIMIT),
        cost_estimate=cost(5),
        name="hidden",
    )(states, scale)


def phase(*values):
    return lax.optimization_barrier(values)


def cost(micros):
    return pl.CostEstimate(flops=int(micros * 1e3 * COST), bytes_accessed=1024, transcendentals=0)


def here():
    t = lax.axis_index("tm")
    return lax.axis_index("group"), t, lax.axis_index("tensor"), t % 2


def move(sources, place, sems):
    copies = [pltpu.make_async_copy(src, dst, sems.at[n]) for n, (src, dst) in enumerate(zip(sources, place))]
    for copy in copies:
        copy.start()
    return copies


def params():
    return pltpu.CompilerParams(vmem_limit_bytes=VMEM_LIMIT)


def first_kernel(wq, wk, wv, mine, theirs, a, b, sems):
    g, _, _, core = here()
    half = a.shape[0]
    row = pl.multiple_of(g * half, 16)
    chunks = wq.shape[1] // (2 * HD)
    waits = []
    for m, (buf, out, who) in enumerate(((a, mine, core), (b, theirs, 1 - core))):
        col = pl.multiple_of(who * (chunks * HD), HD)
        src = [w.at[pl.ds(row, half), pl.ds(col, HD)] for w in (wq, wk, wv)]
        dst = [buf.at[:, n * HD : (n + 1) * HD] for n in range(3)]
        waits.append(move(src, dst, sems.at[pl.ds(4 * m, 3)]))
    for m, (buf, out) in enumerate(((a, mine), (b, theirs))):
        for copy in waits[m]:
            copy.wait()
        pltpu.make_async_copy(buf, out, sems.at[4 * m + 3]).start()
    for m, (buf, out) in enumerate(((a, mine), (b, theirs))):
        pltpu.make_async_copy(buf, out, sems.at[4 * m + 3]).wait()


def first_packs(weights):
    half = weights[0].shape[0] // 2
    shape = (half, 3 * HD)
    return pl.pallas_call(
        first_kernel,
        in_specs=[ANY] * 3,
        out_specs=[ANY] * 2,
        out_shape=[jax.ShapeDtypeStruct(shape, jnp.bfloat16)] * 2,
        scratch_shapes=[pltpu.VMEM(shape, jnp.bfloat16)] * 2 + [pltpu.SemaphoreType.DMA((8,))],
        compiler_params=params(),
        cost_estimate=cost(1),
        name="first_packs",
    )(*weights)


def packs_kernel(wq, wk, wv, pq, pk, pv, w_out, *refs):
    chunks = wq.shape[1] // (2 * HD)
    outs, bufs, (sems,) = refs[: chunks + 1], refs[chunks + 1 : 2 * (chunks + 1)], refs[2 * (chunks + 1) :]
    g, _, z, core = here()
    half = wq.shape[0] // 2
    share = w_out.shape[1] // 2
    row = pl.multiple_of(g * half, 16)
    waits = []
    for j in range(1, chunks):
        col = pl.multiple_of(core * (chunks * HD) + j * HD, HD)
        src = [w.at[pl.ds(row, half), pl.ds(col, HD)] for w in (wq, wk, wv, pq, pk, pv)]
        dst = [
            bufs[j - 1].at[(n // 3) * half : (n // 3 + 1) * half, (n % 3) * HD : (n % 3 + 1) * HD] for n in range(6)
        ]
        waits.append(move(src, dst, sems.at[pl.ds(6 * (j - 1), 6)]))
    base = 6 * (chunks - 1)
    for k in range(2):
        at = pl.multiple_of((k ^ (z // 2)) * share, HD)
        waits.append(move([w_out.at[:, pl.ds(at, share)]], [bufs[chunks - 1 + k]], sems.at[pl.ds(base + k, 1)]))
    for n, copies in enumerate(waits):
        for copy in copies:
            copy.wait()
        pltpu.make_async_copy(bufs[n], outs[n], sems.at[base + 2 + n]).start()
    for n in range(chunks + 1):
        pltpu.make_async_copy(bufs[n], outs[n], sems.at[base + 2 + n]).wait()


def packs(own, partner, w_out):
    depth, cols = own[0].shape
    chunks = cols // (2 * HD)
    shapes = [(depth, 3 * HD)] * (chunks - 1) + [(w_out.shape[0], w_out.shape[1] // 2)] * 2
    return pl.pallas_call(
        packs_kernel,
        in_specs=[ANY] * 7,
        out_specs=[ANY] * len(shapes),
        out_shape=[jax.ShapeDtypeStruct(shape, jnp.bfloat16) for shape in shapes],
        scratch_shapes=[pltpu.VMEM(shape, jnp.bfloat16) for shape in shapes]
        + [pltpu.SemaphoreType.DMA((6 * (chunks - 1) + 2 + len(shapes),))],
        compiler_params=params(),
        cost_estimate=cost(1),
        name="packs",
    )(*own, *partner, w_out)


def near_kernel(h_own, h_par, wq, wk, wv, pq, pk, pv, out, hbuf, wbuf, obuf, hsems, wsems, osems):
    _, t, _, core = here()
    depth = wq.shape[0]
    chunks = wq.shape[1] // (2 * HD)
    wide = chunks * HD
    head = pl.multiple_of(core * wide, HD)
    spans = [slice(m * depth, (m + 1) * depth) for m in range(2)]
    at = [pl.multiple_of(owner * depth, HD) for owner in (t, t ^ 1)]

    def hidden_part(i, h):
        src = [h.at[:, pl.ds(at[m], depth)] for m in range(2)]
        return move(src, [hbuf.at[i, :, spans[m]] for m in range(2)], hsems.at[pl.ds(2 * i, 2)])

    hcopies = [hidden_part(0, h_own)]
    wcopies = []
    for n, pair in enumerate(((wq, pq), (wk, pk), (wv, pv))):
        src = [w.at[:, pl.ds(head, wide)] for w in pair]
        dst = [wbuf.at[spans[m], n * wide : (n + 1) * wide] for m in range(2)]
        wcopies.append(move(src, dst, wsems.at[pl.ds(2 * n, 2)]))
    hcopies.append(hidden_part(1, h_par))
    cols = 3 * wide
    last = []
    for i in range(2):
        for copy in hcopies[i]:
            copy.wait()
        ready = 0
        for low in range(0, cols, 256):
            tile = slice(low, min(low + 256, cols))
            while i == 0 and ready * wide < tile.stop:
                for copy in wcopies[ready]:
                    copy.wait()
                ready += 1
            obuf[i, :, tile] = jnp.dot(hbuf[i], wbuf[:, tile], preferred_element_type=jnp.float32)
        src = [obuf.at[i, :, n * wide + j * HD : n * wide + (j + 1) * HD] for j in range(chunks) for n in range(3)]
        dst = [out.at[j, i, :, n * HD : (n + 1) * HD] for j in range(chunks) for n in range(3)]
        last += move(src, dst, osems.at[pl.ds(i * 3 * chunks, 3 * chunks)])
    for copy in last:
        copy.wait()


def near(hidden, beside, weights):
    rows, _ = hidden.shape
    depth, cols = weights[0].shape
    chunks = cols // (2 * HD)
    return pl.pallas_call(
        near_kernel,
        in_specs=[ANY] * 8,
        out_specs=ANY,
        out_shape=jax.ShapeDtypeStruct((chunks, 2, rows, 3 * HD), jnp.float32),
        scratch_shapes=[
            pltpu.VMEM((2, rows, 2 * depth), jnp.bfloat16),
            pltpu.VMEM((2 * depth, 3 * HD * chunks), jnp.bfloat16),
            pltpu.VMEM((2, rows, 3 * HD * chunks), jnp.float32),
            pltpu.SemaphoreType.DMA((4,)),
            pltpu.SemaphoreType.DMA((6,)),
            pltpu.SemaphoreType.DMA((6 * chunks,)),
        ],
        compiler_params=params(),
        cost_estimate=cost(10),
        name="near",
    )(hidden, beside, *weights)


def attend_kernel(chunk, row, parts, h_own, h_par, acc, qg, kg, *refs):
    pieces, (out, hbuf, wbuf, abuf, hsems, wsems, asems) = refs[:parts], refs[parts:]
    g, t, _, core = here()
    rows = hbuf.shape[1]
    half = hbuf.shape[2] // 4
    tall = 4 * half // parts
    chunks = qg.shape[1] // (2 * HD)
    starts = [(t ^ (2 + n % 2)) * (2 * half) + (g if n < 2 else 1 - g) * half for n in range(4)]
    wcopies, hcopies, acopies = [], [[], []], []
    for part in range(2):
        some = range(part * parts // 2, (part + 1) * parts // 2)
        dst = [wbuf.at[n * tall : (n + 1) * tall, :] for n in some]
        wcopies.append(move([pieces[n] for n in some], dst, wsems.at[pl.ds(part * parts // 2, parts // 2)]))
        for i, h in enumerate((h_own, h_par)):
            src = [h.at[:, pl.ds(pl.multiple_of(starts[n], HD), half)] for n in (2 * part, 2 * part + 1)]
            dst = [hbuf.at[i, :, n * half : (n + 1) * half] for n in (2 * part, 2 * part + 1)]
            hcopies[i].append(move(src, dst, hsems.at[pl.ds(4 * i + 2 * part, 2)]))
            if part == 0:
                acopies += move([acc.at[row, i]], [abuf.at[i]], asems.at[pl.ds(i, 1)])
    head = pl.multiple_of(core * (chunks * HD) + chunk * HD, HD)

    def normed(values, gain):
        scale = lax.rsqrt(jnp.mean(values * values, axis=-1, keepdims=True) + 1e-06)
        return (values * scale * gain).astype(jnp.bfloat16)

    block = rows // 2
    for i in range(2):
        for part in range(2):
            if i == 0:
                for copy in wcopies[part]:
                    copy.wait()
            for copy in hcopies[i][part]:
                copy.wait()
            if part == 0:
                acopies[i].wait()
            span = slice(2 * part * half, 2 * (part + 1) * half)
            abuf[i] += jnp.dot(hbuf[i, :, span], wbuf[span, :], preferred_element_type=jnp.float32)
        qn = normed(abuf[i, :, :HD], qg[:, pl.ds(head, HD)])
        kn = normed(abuf[i, :, HD : 2 * HD], kg[:, pl.ds(head, HD)])
        vb = abuf[i, :, 2 * HD :].astype(jnp.bfloat16)
        for r in range(2):
            scores = lax.dot_general(
                qn[r * block : (r + 1) * block],
                kn,
                (((1,), (1,)), ((), ())),
                preferred_element_type=jnp.float32,
            )
            top = jnp.max(scores, axis=-1, keepdims=True)
            grown = jnp.exp2((scores - top) * (math.log2(math.e) / math.sqrt(HD)))
            probs = grown * (1.0 / jnp.sum(grown, axis=-1, keepdims=True))
            out[i, r * block : (r + 1) * block, :] = jnp.dot(
                probs.astype(jnp.bfloat16), vb, preferred_element_type=jnp.float32
            ).astype(jnp.bfloat16)


def attend(chunk, hidden, beside, acc, row, pieces, qg, kg):
    rows = hidden.shape[0]
    parts = len(pieces)
    depth = sum(p.shape[0] for p in pieces)
    return pl.pallas_call(
        functools.partial(attend_kernel, chunk, row, parts),
        in_specs=[FREE] * 3 + [VMEM] * 2 + [FREE] * parts,
        out_specs=VMEM,
        out_shape=jax.ShapeDtypeStruct((2, rows, HD), jnp.bfloat16),
        scratch_shapes=[
            pltpu.VMEM((2, rows, depth), jnp.bfloat16),
            pltpu.VMEM((depth, 3 * HD), jnp.bfloat16),
            pltpu.VMEM((2, rows, 3 * HD), jnp.float32),
            pltpu.SemaphoreType.DMA((8,)),
            pltpu.SemaphoreType.DMA((parts,)),
            pltpu.SemaphoreType.DMA((2,)),
        ],
        compiler_params=params(),
        cost_estimate=cost(12),
        name="attend",
    )(hidden, beside, acc, qg.reshape(1, -1), kg.reshape(1, -1), *pieces)


def bundle_kernel(count, *refs):
    pieces, (out, buf, sems) = refs[:count], refs[count:]
    copies = move(pieces[:3], [buf.at[d] for d in range(3)], sems.at[pl.ds(0, 3)])
    copies.append(pltpu.make_async_copy(pieces[3], buf.at[3], sems.at[3]))
    if count == 4:
        copies[3].start()
    else:
        _, _, z, _ = here()
        inner = jnp.logical_or(z == 1, z == 2)
        pl.when(inner)(copies[3].start)
        pl.when(jnp.logical_not(inner))(pltpu.make_async_copy(pieces[4], buf.at[3], sems.at[3]).start)
    for d, copy in enumerate(copies):
        copy.wait()
        pltpu.make_async_copy(buf.at[d], out.at[d], sems.at[4 + d]).start()
    for d in range(4):
        pltpu.make_async_copy(buf.at[d], out.at[d], sems.at[4 + d]).wait()


def bundle(*pieces):
    shape = (4, *pieces[0].shape)
    return pl.pallas_call(
        functools.partial(bundle_kernel, len(pieces)),
        in_specs=[ANY] * len(pieces),
        out_specs=ANY,
        out_shape=jax.ShapeDtypeStruct(shape, pieces[0].dtype),
        scratch_shapes=[pltpu.VMEM(shape, pieces[0].dtype), pltpu.SemaphoreType.DMA((8,))],
        compiler_params=params(),
        cost_estimate=cost(1),
        name="bundle",
    )(*pieces)


def out_kernel(chunks, top, gate_own, gate_par, *refs):
    mine, theirs, refs = refs[: chunks - 1], refs[chunks - 1 : 2 * chunks - 2], refs[2 * chunks - 2 :]
    last_mine, last_theirs, pieces = refs[:4], refs[4:8], refs[8:12]
    terms, total, att, w, asems, wsems = refs[12:]
    devices, _, rows, _ = att.shape
    group, _, plane, core = here()
    span = slice(top, top + rows)
    waits = []
    for d in range(devices):
        pairs = []
        for j in range(chunks):
            got, given = (mine[j].at[d], theirs[j].at[d]) if j < chunks - 1 else (last_mine[d], last_theirs[d])
            at = pl.multiple_of(core * (chunks * HD) + j * HD, HD)
            pairs.append((got.at[:, span, :], att.at[d, :, :, pl.ds(at, HD)]))
            at = pl.multiple_of((1 - core) * (chunks * HD) + j * HD, HD)
            for i in range(2):
                pairs.append((given.at[1 - i, span, :], att.at[d, i, :, pl.ds(at, HD)]))
        waits.append([pltpu.make_async_copy(a, b, asems.at[3 * chunks * d + n]) for n, (a, b) in enumerate(pairs)])
    wcopies = []
    for d in range(devices):
        block = plane ^ d
        slot = (block // 2) ^ core
        swap = (block % 2) ^ group
        which = 2 * slot + swap
        for n, piece in enumerate(pieces):
            copy = pltpu.make_async_copy(piece, w.at[d], wsems.at[d])
            pl.when(which == n)(copy.start)
        wcopies.append(pltpu.make_async_copy(pieces[0], w.at[d], wsems.at[d]))
        for copy in waits[d]:
            copy.start()
    for d in range(devices):
        wcopies[d].wait()
        for copy in waits[d]:
            copy.wait()
        for i, gate in enumerate((gate_own, gate_par)):
            place = core if i == 0 else 1 - core
            part = (
                jnp.dot(att[d, i], w[d], preferred_element_type=jnp.float32).astype(jnp.bfloat16).astype(jnp.float32)
            )
            if d > 0:
                part = terms[place] + part
            if d == devices - 1:
                part = gate[...] * part
            terms[place] = part
    total[...] = (terms[0] + terms[1]).astype(total.dtype)


def out_projection(top, count, gate_own, gate_par, mine, theirs, last_mine, last_theirs, pieces):
    chunks = len(mine) + 1
    devices = mine[0].shape[0]
    deep, share = pieces[0].shape
    return pl.pallas_call(
        functools.partial(out_kernel, chunks, top),
        in_specs=[VMEM, VMEM] + [FREE] * (2 * chunks + 10),
        out_specs=[VMEM, VMEM],
        out_shape=[
            jax.ShapeDtypeStruct((2, count, share), jnp.float32),
            jax.ShapeDtypeStruct((count, share), CARRY),
        ],
        scratch_shapes=[
            pltpu.VMEM((devices, 2, count, deep), jnp.bfloat16),
            pltpu.VMEM((devices, deep, share), jnp.bfloat16),
            pltpu.SemaphoreType.DMA((devices * 3 * chunks,)),
            pltpu.SemaphoreType.DMA((devices,)),
        ],
        compiler_params=params(),
        cost_estimate=cost(12),
        name="out_projection",
    )(gate_own, gate_par, *mine, *theirs, *last_mine, *last_theirs, *pieces)


def close_kernel(terms, carry, far, own, par, mine, send, squares):
    _, t, _, core = here()
    first = core == 0
    low = jnp.where(first, own[...], par[...]).astype(jnp.float32)
    high = jnp.where(first, par[...], own[...]).astype(jnp.float32)
    at_low = jnp.where(t < 2, low, far[...].astype(jnp.float32)) + carry[...].astype(jnp.float32)
    at_high = at_low + terms[0]
    end = at_high + terms[1]
    mine[...] = jnp.where(first, at_high, end)
    send[...] = jnp.where(first, end, at_high)
    for n, gap in enumerate((at_low - low, at_high - high)):
        part = jnp.sum(gap * gap, axis=0, keepdims=True)

        @pl.when(pl.program_id(0) == 0)
        def _(n=n, part=part):
            squares[n : n + 1, :] = part

        @pl.when(pl.program_id(0) > 0)
        def _(n=n, part=part):
            squares[n : n + 1, :] += part


def close(top, terms, carry, far, own, par):
    _, count, share = terms.shape
    block = 192 if count % 192 == 0 and top % 192 == 0 else count
    skip = top // block
    whole = pl.BlockSpec((block, share), lambda i: (skip + i, 0))
    part = pl.BlockSpec((block, share), lambda i: (i, 0))
    return pl.pallas_call(
        close_kernel,
        grid=(count // block,),
        in_specs=[pl.BlockSpec((2, block, share), lambda i: (0, i, 0)), part, whole, whole, whole],
        out_specs=[part, part, pl.BlockSpec((2, share), lambda i: (0, 0))],
        out_shape=[
            jax.ShapeDtypeStruct((count, share), jnp.float32),
            jax.ShapeDtypeStruct((count, share), jnp.float32),
            jax.ShapeDtypeStruct((2, share), jnp.float32),
        ],
        compiler_params=params(),
        cost_estimate=cost(8),
        name="close",
    )(terms, carry, far, own, par)


def join_kernel(parts, *refs):
    mine, given, (out, buf, sems) = refs[:parts], refs[parts : 2 * parts], refs[2 * parts :]
    count, share = mine[0].shape
    _, _, _, core = here()
    copies = []
    for n, piece in enumerate((*mine, *given)):
        rows = slice((n % parts) * count, (n % parts + 1) * count)
        at = pl.multiple_of((core if n < parts else 1 - core) * share, HD)
        copies.append(
            (
                pltpu.make_async_copy(piece, buf.at[n], sems.at[2 * n]),
                pltpu.make_async_copy(buf.at[n], out.at[0, rows, pl.ds(at, share)], sems.at[2 * n + 1]),
            )
        )
    for come, _ in copies:
        come.start()
    for come, go in copies:
        come.wait()
        go.start()
    for _, go in copies:
        go.wait()


def join(mine, given):
    parts = len(mine)
    count, share = mine[0].shape
    return pl.pallas_call(
        functools.partial(join_kernel, parts),
        in_specs=[FREE] * (2 * parts),
        out_specs=ANY,
        out_shape=jax.ShapeDtypeStruct((1, parts * count, 2 * share), jnp.float32),
        scratch_shapes=[
            pltpu.VMEM((2 * parts, count, share), jnp.float32),
            pltpu.SemaphoreType.DMA((4 * parts,)),
        ],
        compiler_params=params(),
        cost_estimate=cost(8),
        name="join",
    )(*mine, *given)


def fast_body(
    states, timesteps, step_sizes, mod_scale, mod_gate, w_query, w_key, w_value, query_gain, key_gain, w_out
):
    latent = states[0]
    rows, width = latent.shape
    stamp = timesteps[0].astype(jnp.float32)
    t, z = lax.axis_index("tm"), lax.axis_index("tensor")
    core, chip = t % 2, t // 2
    devices = 4
    steps = range(4)
    share = mod_gate.shape[0] // 2
    chunks = w_query.shape[1] // (2 * HD)

    def over(array, axis, flip):
        return lax.ppermute(array, axis, [(i, i ^ flip) for i in range(lax.axis_size(axis))])

    def far(array):
        return over(array, "tm", 2)

    def swap(array):
        return over(array, "group", 1)

    def partner(array):
        return over(array, "tm", 1)

    def along(array, flip):
        return over(array, "tensor", flip)

    def middle(array):
        return lax.ppermute(array, "tensor", [(1, 2), (2, 1)])

    def outward(array):
        return lax.ppermute(array, "tensor", [(1, 0), (2, 3)])

    def place(group, step, tensor):
        return (group * 4 + step) * devices + tensor

    def cross(array):
        pairs = [(a * devices + b, (a ^ 2) * devices + b) for a in steps for b in range(devices) if a // 2 == b // 2]
        return lax.ppermute(array, ("tm", "tensor"), pairs)

    def to_plane(k, piece):
        pairs = [
            (place(b % 2, a, b), place(b % 2, 2 * (a // 2) + (k ^ (b // 2)), a))
            for a in steps
            for b in range(devices)
        ]
        return lax.ppermute(piece, ("group", "tm", "tensor"), pairs)

    weights = (w_query, w_key, w_value)
    others = [partner(w) for w in weights]
    own_step = jnp.stack([stamp, step_sizes[0]])
    par_step = partner(own_step)
    p0, r0 = first_packs(weights)
    p0, r0, w_out, states = phase(p0, r0, w_out, states)

    y0 = far(p0)
    z0 = over(r0, "tm", 3)
    base = z * (2 * share)
    lat_own = lax.dynamic_slice_in_dim(states[0], base + core * share, share, 1)
    lat_give = lax.dynamic_slice_in_dim(states[0], base + (1 - core) * share, share, 1)
    lat_par = partner(lat_give)
    hidden = fast_hidden(states, make_scale(stamp, mod_scale))
    s1, s2, o0, o1 = packs(weights, others, w_out)
    y0, z0, hidden, s1, s2, o0, o1, lat_own, lat_par, own_step, par_step = phase(
        y0, z0, hidden, s1, s2, o0, o1, lat_own, lat_par, own_step, par_step
    )

    beside = partner(hidden)
    y1, x0, xz0, sent0, sent1 = far(s1), swap(y0), swap(z0), to_plane(0, o0), to_plane(1, o1)
    acc = near(hidden, beside, (*weights, *others))
    y1, x0, xz0, acc, beside, s2, sent0 = phase(y1, x0, xz0, acc, beside, s2, sent0)

    x1, y2 = swap(y1), far(s2)
    att0 = attend(0, hidden, beside, acc, 0, (y0, z0, x0, xz0), query_gain, key_gain)
    att0, own_step, par_step, sent1 = phase(att0, own_step, par_step, sent1)
    two0, one0 = along(att0, 2), along(att0, 1)
    gates = []
    for pair in (own_step, par_step):
        gate = pair[1] * make_gate(pair[0], mod_gate, width)
        gates.append(lax.dynamic_slice_in_dim(gate, core * share, share, 0).reshape(1, share))
    y2, x1, acc, *gates = phase(y2, x1, acc, *gates)

    x2, u0, inner0 = swap(y2), cross(sent0), middle(att0)
    att1 = attend(1, hidden, beside, acc, 1, (y1, x1), query_gain, key_gain)
    att1, two0, v0 = phase(att1, two0, sent0)
    outer0, two1 = outward(two0), along(att1, 2)
    u0, x2, one0, inner0, outer0, v0 = phase(u0, x2, one0, inner0, outer0, v0)

    home = chip == z // 2
    v0 = jnp.where(home, v0, u0)
    xv0, u1 = swap(v0), cross(sent1)
    one1, inner1 = along(att1, 1), middle(att1)
    att2 = attend(2, hidden, beside, acc, 2, (y2, x2), query_gain, key_gain)
    two1, att2 = phase(two1, att2)
    outer1, two2 = outward(two1), along(att2, 2)
    g0 = bundle(att0, one0, two0, inner0, outer0)
    u1, xv0, v0, one1, inner1, outer1, g0, lat_own, lat_par, *gates = phase(
        u1, xv0, v0, one1, inner1, outer1, g0, lat_own, lat_par, *gates
    )
    gate_own, gate_par = gates

    one2 = along(att2, 1)
    v1 = jnp.where(home, sent1, u1)
    xv1 = swap(v1)
    start_far = lax.ppermute(jnp.where(core == 0, lat_own, lat_par), "tm", [(0, 2), (1, 3)])
    g1 = bundle(att1, one1, two1, inner1, outer1)
    two2, one2, v1, xv1, g1, start_far = phase(two2, one2, v1, xv1, g1, start_far)
    outer2, inner2 = outward(two2), middle(att2)
    q0, q1, b0, b1, b2 = partner(g0), partner(g1), partner(att2), partner(one2), partner(two2)
    outer2, inner2, q0, q1, b0, b1, b2 = phase(outer2, inner2, q0, q1, b0, b1, b2)

    three2 = jnp.where(jnp.logical_or(z == 1, z == 2), inner2, outer2)
    b3 = partner(three2)
    pieces = [v0, xv0, v1, xv1]

    count = rows // 2

    def project(top, gate_own):
        mine, theirs = [att2, one2, two2, three2], [b0, b1, b2, b3]
        return out_projection(top, count, gate_own, gate_par, [g0, g1], [q0, q1], mine, theirs, pieces)

    def ahead(total):
        return lax.ppermute(total, "tm", [(0, 2), (1, 3)])

    terms0, total0 = project(0, gate_own)
    terms0, total0, gate_own = phase(terms0, total0, gate_own)
    carry0 = ahead(total0)
    terms1, total1 = project(count, gate_own)
    terms1, total1, terms0 = phase(terms1, total1, terms0)
    carry1 = ahead(total1)
    own0, send0, squares0 = close(0, terms0, carry0, start_far, lat_own, lat_par)
    carry1, own0, send0, squares0 = phase(carry1, own0, send0, squares0)
    given0 = partner(send0)
    own1, send1, squares1 = close(count, terms1, carry1, start_far, lat_own, lat_par)
    given0, own1, send1, squares = phase(given0, own1, send1, squares0 + squares1)
    given1, squares_par = partner(send1), partner(squares)
    given1, squares = phase(given1, squares + squares_par)
    sums = jnp.sum(squares, axis=1)
    sums = sums + along(sums, 1) + along(sums, 2) + along(sums, 3)
    next_share = join([own0, own1], [given0, given1])
    errors = (lax.dynamic_slice_in_dim(sums, core, 1, 0) / (rows * width)).reshape(1, 1)
    return (next_share, errors)


def solution(mesh):
    placed = (
        P("tm", "group", None),
        P("tm"),
        P("tm"),
        P(),
        P("tensor"),
        P("tm", "tensor"),
        P("tm", "tensor"),
        P("tm", "tensor"),
        P("tensor"),
        P("tensor"),
        P("tensor", "tm"),
    )
    fast = mesh.shape["group"] == 2 and mesh.shape["tm"] == 4 and mesh.shape["tensor"] == 4
    return jax.shard_map(
        fast_body if fast else general_body,
        mesh=mesh,
        in_specs=placed,
        out_specs=(P("tm", "group", "tensor"), P("group", "tm")),
        check_vma=False,
    )
```

```python
import functools
import math

import jax
import jax.numpy as jnp
from jax import lax
from jax.experimental import pallas as pl
from jax.experimental.pallas import tpu as pltpu
from jax.sharding import PartitionSpec as P

HD = 128
CARRY = jnp.bfloat16
COST = 3e6
VMEM_LIMIT = 56 * 2**20
ANY = pl.BlockSpec(memory_space=pltpu.HBM)
FREE = pl.BlockSpec(memory_space=pl.ANY)
VMEM = pl.BlockSpec(memory_space=pltpu.VMEM)


def spread(block, axis, holder):
    block = jnp.where(lax.axis_index(axis) == holder, block, jnp.zeros_like(block))
    return lax.psum(block, axis)


def from_behind(array, axis, by):
    devices = lax.axis_size(axis)
    pairs = [(i, i + by) for i in range(devices) if 0 <= i + by < devices]
    return lax.ppermute(array, axis, pairs)


def head_norm(values, gain):
    rows = values.shape[0]
    count = values.shape[1] // HD
    split = values.reshape(rows, count, HD)
    normed = split * lax.rsqrt(jnp.mean(split * split, axis=-1, keepdims=True) + 1e-06)
    return (normed * gain.reshape(count, HD)).astype(jnp.bfloat16)


def make_hidden(latent, stamp, mod_scale):
    width = latent.shape[1]
    omega = jnp.exp(-math.log(10000.0) * jnp.arange(width).astype(jnp.float32) / width)
    values = latent.astype(jnp.float32)
    normed = values * lax.rsqrt(jnp.mean(values * values, axis=-1, keepdims=True) + 1e-06)
    return (normed * (1.0 + mod_scale * jnp.cos(stamp * omega))).astype(jnp.bfloat16)


def make_gate(stamp, mod_gate, width):
    share = mod_gate.shape[0]
    offset = lax.axis_index("tensor") * share
    positions = (offset + jnp.arange(share)).astype(jnp.float32)
    omega_share = jnp.exp(-math.log(10000.0) * positions / width)
    return 1.0 + mod_gate * jnp.sin(stamp * omega_share)


def general_body(
    states, timesteps, step_sizes, mod_scale, mod_gate, w_query, w_key, w_value, query_gain, key_gain, w_out
):
    latent = states[0]
    rows, width = latent.shape
    stamp = timesteps[0].astype(jnp.float32)
    hidden = make_hidden(latent, stamp, mod_scale)
    local_heads = w_query.shape[1]

    def project(weight):
        whole = lax.all_gather(weight, "tm", axis=0, tiled=True)
        return jnp.dot(hidden, whole, preferred_element_type=jnp.float32)

    count = local_heads // HD
    q_norm = head_norm(project(w_query), query_gain)
    k_norm = head_norm(project(w_key), key_gain)
    v_heads = project(w_value).astype(jnp.bfloat16).reshape(rows, count, HD)
    scores = jnp.einsum("qhd,khd->hqk", q_norm, k_norm, preferred_element_type=jnp.float32) / math.sqrt(HD)
    probs = jax.nn.softmax(scores, axis=-1).astype(jnp.bfloat16)
    attended = jnp.einsum("hqk,khd->qhd", probs, v_heads, preferred_element_type=jnp.float32)
    attended = attended.astype(jnp.bfloat16).reshape(rows, local_heads)
    share = mod_gate.shape[0]
    offset = lax.axis_index("tensor") * share
    partial_out = jnp.dot(
        attended,
        lax.all_gather(w_out, "tm", axis=1, tiled=True),
        preferred_element_type=jnp.float32,
    )
    projected = lax.psum_scatter(
        partial_out.astype(jnp.bfloat16), "tensor", scatter_dimension=1, tiled=True
    ).astype(jnp.float32)
    term = step_sizes[0] * make_gate(stamp, mod_gate, width) * projected
    own_slice = lax.dynamic_slice_in_dim(latent, offset, share, 1)
    own_start = own_slice.astype(jnp.float32)
    base_state = spread(own_slice, "tm", 0).astype(jnp.float32)
    running = term
    for level in range((lax.axis_size("tm") - 1).bit_length()):
        running = running + from_behind(running, "tm", 1 << level)
    before = running - term
    predicted = base_state + before
    next_share = predicted + term
    gap = predicted - own_start
    squared = lax.psum(jnp.sum(gap * gap), "tensor")
    errors = (squared / (rows * width)).reshape(1, 1)
    return (next_share[None], errors)


def after(value, *others):
    return lax.optimization_barrier((value, *others))[0]


def hidden_kernel(latent, scale, out):
    values = latent[0].astype(jnp.float32)
    normed = values * lax.rsqrt(jnp.mean(values * values, axis=-1, keepdims=True) + 1e-06)
    out[...] = (normed * scale[...]).astype(jnp.bfloat16)


def make_scale(stamp, mod_scale):
    width = mod_scale.shape[0]
    omega = jnp.exp(-math.log(10000.0) * jnp.arange(width).astype(jnp.float32) / width)
    return (1.0 + mod_scale * jnp.cos(stamp * omega)).reshape(1, width)


def fast_hidden(states, scale):
    _, rows, width = states.shape
    block = 192 if rows % 192 == 0 else rows
    return pl.pallas_call(
        hidden_kernel,
        grid=(rows // block,),
        in_specs=[
            pl.BlockSpec((1, block, width), lambda i: (0, i, 0)),
            pl.BlockSpec((1, width), lambda i: (0, 0)),
        ],
        out_specs=pl.BlockSpec((block, width), lambda i: (i, 0)),
        out_shape=jax.ShapeDtypeStruct((rows, width), jnp.bfloat16),
        compiler_params=pltpu.CompilerParams(vmem_limit_bytes=VMEM_LIMIT),
        cost_estimate=cost(5),
        name="hidden",
    )(states, scale)


def phase(*values):
    return lax.optimization_barrier(values)


def cost(micros):
    return pl.CostEstimate(flops=int(micros * 1e3 * COST), bytes_accessed=1024, transcendentals=0)


def here():
    t = lax.axis_index("tm")
    return lax.axis_index("group"), t, lax.axis_index("tensor"), t % 2


def move(sources, place, sems):
    copies = [pltpu.make_async_copy(src, dst, sems.at[n]) for n, (src, dst) in enumerate(zip(sources, place))]
    for copy in copies:
        copy.start()
    return copies


def params():
    return pltpu.CompilerParams(vmem_limit_bytes=VMEM_LIMIT)


def first_kernel(wq, wk, wv, mine, theirs, a, b, sems):
    g, _, _, core = here()
    half = a.shape[0]
    row = pl.multiple_of(g * half, 16)
    chunks = wq.shape[1] // (2 * HD)
    waits = []
    for m, (buf, out, who) in enumerate(((a, mine, core), (b, theirs, 1 - core))):
        col = pl.multiple_of(who * (chunks * HD), HD)
        src = [w.at[pl.ds(row, half), pl.ds(col, HD)] for w in (wq, wk, wv)]
        dst = [buf.at[:, n * HD : (n + 1) * HD] for n in range(3)]
        waits.append(move(src, dst, sems.at[pl.ds(4 * m, 3)]))
    for m, (buf, out) in enumerate(((a, mine), (b, theirs))):
        for copy in waits[m]:
            copy.wait()
        pltpu.make_async_copy(buf, out, sems.at[4 * m + 3]).start()
    for m, (buf, out) in enumerate(((a, mine), (b, theirs))):
        pltpu.make_async_copy(buf, out, sems.at[4 * m + 3]).wait()


def first_packs(weights):
    half = weights[0].shape[0] // 2
    shape = (half, 3 * HD)
    return pl.pallas_call(
        first_kernel,
        in_specs=[ANY] * 3,
        out_specs=[ANY] * 2,
        out_shape=[jax.ShapeDtypeStruct(shape, jnp.bfloat16)] * 2,
        scratch_shapes=[pltpu.VMEM(shape, jnp.bfloat16)] * 2 + [pltpu.SemaphoreType.DMA((8,))],
        compiler_params=params(),
        cost_estimate=cost(1),
        name="first_packs",
    )(*weights)


def packs_kernel(wq, wk, wv, pq, pk, pv, w_out, *refs):
    chunks = wq.shape[1] // (2 * HD)
    outs, bufs, (sems,) = refs[: chunks + 1], refs[chunks + 1 : 2 * (chunks + 1)], refs[2 * (chunks + 1) :]
    g, _, z, core = here()
    half = wq.shape[0] // 2
    share = w_out.shape[1] // 2
    row = pl.multiple_of(g * half, 16)
    waits = []
    for j in range(1, chunks):
        col = pl.multiple_of(core * (chunks * HD) + j * HD, HD)
        src = [w.at[pl.ds(row, half), pl.ds(col, HD)] for w in (wq, wk, wv, pq, pk, pv)]
        dst = [
            bufs[j - 1].at[(n // 3) * half : (n // 3 + 1) * half, (n % 3) * HD : (n % 3 + 1) * HD] for n in range(6)
        ]
        waits.append(move(src, dst, sems.at[pl.ds(6 * (j - 1), 6)]))
    base = 6 * (chunks - 1)
    for k in range(2):
        at = pl.multiple_of((k ^ (z // 2)) * share, HD)
        waits.append(move([w_out.at[:, pl.ds(at, share)]], [bufs[chunks - 1 + k]], sems.at[pl.ds(base + k, 1)]))
    for n, copies in enumerate(waits):
        for copy in copies:
            copy.wait()
        pltpu.make_async_copy(bufs[n], outs[n], sems.at[base + 2 + n]).start()
    for n in range(chunks + 1):
        pltpu.make_async_copy(bufs[n], outs[n], sems.at[base + 2 + n]).wait()


def packs(own, partner, w_out):
    depth, cols = own[0].shape
    chunks = cols // (2 * HD)
    shapes = [(depth, 3 * HD)] * (chunks - 1) + [(w_out.shape[0], w_out.shape[1] // 2)] * 2
    return pl.pallas_call(
        packs_kernel,
        in_specs=[ANY] * 7,
        out_specs=[ANY] * len(shapes),
        out_shape=[jax.ShapeDtypeStruct(shape, jnp.bfloat16) for shape in shapes],
        scratch_shapes=[pltpu.VMEM(shape, jnp.bfloat16) for shape in shapes]
        + [pltpu.SemaphoreType.DMA((6 * (chunks - 1) + 2 + len(shapes),))],
        compiler_params=params(),
        cost_estimate=cost(1),
        name="packs",
    )(*own, *partner, w_out)


def near_kernel(h_own, h_par, wq, wk, wv, pq, pk, pv, out, hbuf, wbuf, obuf, hsems, wsems, osems):
    _, t, _, core = here()
    depth = wq.shape[0]
    chunks = wq.shape[1] // (2 * HD)
    wide = chunks * HD
    head = pl.multiple_of(core * wide, HD)
    spans = [slice(m * depth, (m + 1) * depth) for m in range(2)]
    at = [pl.multiple_of(owner * depth, HD) for owner in (t, t ^ 1)]

    def hidden_part(i, h):
        src = [h.at[:, pl.ds(at[m], depth)] for m in range(2)]
        return move(src, [hbuf.at[i, :, spans[m]] for m in range(2)], hsems.at[pl.ds(2 * i, 2)])

    hcopies = [hidden_part(0, h_own)]
    wcopies = []
    for n, pair in enumerate(((wq, pq), (wk, pk), (wv, pv))):
        src = [w.at[:, pl.ds(head, wide)] for w in pair]
        dst = [wbuf.at[spans[m], n * wide : (n + 1) * wide] for m in range(2)]
        wcopies.append(move(src, dst, wsems.at[pl.ds(2 * n, 2)]))
    hcopies.append(hidden_part(1, h_par))
    cols = 3 * wide
    last = []
    for i in range(2):
        for copy in hcopies[i]:
            copy.wait()
        ready = 0
        for low in range(0, cols, 256):
            tile = slice(low, min(low + 256, cols))
            while i == 0 and ready * wide < tile.stop:
                for copy in wcopies[ready]:
                    copy.wait()
                ready += 1
            obuf[i, :, tile] = jnp.dot(hbuf[i], wbuf[:, tile], preferred_element_type=jnp.float32)
        src = [obuf.at[i, :, n * wide + j * HD : n * wide + (j + 1) * HD] for j in range(chunks) for n in range(3)]
        dst = [out.at[j, i, :, n * HD : (n + 1) * HD] for j in range(chunks) for n in range(3)]
        last += move(src, dst, osems.at[pl.ds(i * 3 * chunks, 3 * chunks)])
    for copy in last:
        copy.wait()


def near(hidden, beside, weights):
    rows, _ = hidden.shape
    depth, cols = weights[0].shape
    chunks = cols // (2 * HD)
    return pl.pallas_call(
        near_kernel,
        in_specs=[ANY] * 8,
        out_specs=ANY,
        out_shape=jax.ShapeDtypeStruct((chunks, 2, rows, 3 * HD), jnp.float32),
        scratch_shapes=[
            pltpu.VMEM((2, rows, 2 * depth), jnp.bfloat16),
            pltpu.VMEM((2 * depth, 3 * HD * chunks), jnp.bfloat16),
            pltpu.VMEM((2, rows, 3 * HD * chunks), jnp.float32),
            pltpu.SemaphoreType.DMA((4,)),
            pltpu.SemaphoreType.DMA((6,)),
            pltpu.SemaphoreType.DMA((6 * chunks,)),
        ],
        compiler_params=params(),
        cost_estimate=cost(10),
        name="near",
    )(hidden, beside, *weights)


def attend_kernel(chunk, row, parts, h_own, h_par, acc, qg, kg, *refs):
    pieces, (out, hbuf, wbuf, abuf, hsems, wsems, asems) = refs[:parts], refs[parts:]
    g, t, _, core = here()
    rows = hbuf.shape[1]
    half = hbuf.shape[2] // 4
    tall = 4 * half // parts
    chunks = qg.shape[1] // (2 * HD)
    starts = [(t ^ (2 + n % 2)) * (2 * half) + (g if n < 2 else 1 - g) * half for n in range(4)]
    wcopies, hcopies, acopies = [], [[], []], []
    for part in range(2):
        some = range(part * parts // 2, (part + 1) * parts // 2)
        dst = [wbuf.at[n * tall : (n + 1) * tall, :] for n in some]
        wcopies.append(move([pieces[n] for n in some], dst, wsems.at[pl.ds(part * parts // 2, parts // 2)]))
        for i, h in enumerate((h_own, h_par)):
            src = [h.at[:, pl.ds(pl.multiple_of(starts[n], HD), half)] for n in (2 * part, 2 * part + 1)]
            dst = [hbuf.at[i, :, n * half : (n + 1) * half] for n in (2 * part, 2 * part + 1)]
            hcopies[i].append(move(src, dst, hsems.at[pl.ds(4 * i + 2 * part, 2)]))
            if part == 0:
                acopies += move([acc.at[row, i]], [abuf.at[i]], asems.at[pl.ds(i, 1)])
    head = pl.multiple_of(core * (chunks * HD) + chunk * HD, HD)

    def normed(values, gain):
        scale = lax.rsqrt(jnp.mean(values * values, axis=-1, keepdims=True) + 1e-06)
        return (values * scale * gain).astype(jnp.bfloat16)

    block = rows // 2
    for i in range(2):
        for part in range(2):
            if i == 0:
                for copy in wcopies[part]:
                    copy.wait()
            for copy in hcopies[i][part]:
                copy.wait()
            if part == 0:
                acopies[i].wait()
            span = slice(2 * part * half, 2 * (part + 1) * half)
            abuf[i] += jnp.dot(hbuf[i, :, span], wbuf[span, :], preferred_element_type=jnp.float32)
        qn = normed(abuf[i, :, :HD], qg[:, pl.ds(head, HD)])
        kn = normed(abuf[i, :, HD : 2 * HD], kg[:, pl.ds(head, HD)])
        vb = abuf[i, :, 2 * HD :].astype(jnp.bfloat16)
        for r in range(2):
            scores = lax.dot_general(
                qn[r * block : (r + 1) * block],
                kn,
                (((1,), (1,)), ((), ())),
                preferred_element_type=jnp.float32,
            )
            top = jnp.max(scores, axis=-1, keepdims=True)
            grown = jnp.exp2((scores - top) * (math.log2(math.e) / math.sqrt(HD)))
            probs = grown * (1.0 / jnp.sum(grown, axis=-1, keepdims=True))
            out[i, r * block : (r + 1) * block, :] = jnp.dot(
                probs.astype(jnp.bfloat16), vb, preferred_element_type=jnp.float32
            ).astype(jnp.bfloat16)


def attend(chunk, hidden, beside, acc, row, pieces, qg, kg):
    rows = hidden.shape[0]
    parts = len(pieces)
    depth = sum(p.shape[0] for p in pieces)
    return pl.pallas_call(
        functools.partial(attend_kernel, chunk, row, parts),
        in_specs=[FREE] * 3 + [VMEM] * 2 + [FREE] * parts,
        out_specs=VMEM,
        out_shape=jax.ShapeDtypeStruct((2, rows, HD), jnp.bfloat16),
        scratch_shapes=[
            pltpu.VMEM((2, rows, depth), jnp.bfloat16),
            pltpu.VMEM((depth, 3 * HD), jnp.bfloat16),
            pltpu.VMEM((2, rows, 3 * HD), jnp.float32),
            pltpu.SemaphoreType.DMA((8,)),
            pltpu.SemaphoreType.DMA((parts,)),
            pltpu.SemaphoreType.DMA((2,)),
        ],
        compiler_params=params(),
        cost_estimate=cost(12),
        name="attend",
    )(hidden, beside, acc, qg.reshape(1, -1), kg.reshape(1, -1), *pieces)


def bundle_kernel(count, *refs):
    pieces, (out, buf, sems) = refs[:count], refs[count:]
    copies = move(pieces[:3], [buf.at[d] for d in range(3)], sems.at[pl.ds(0, 3)])
    copies.append(pltpu.make_async_copy(pieces[3], buf.at[3], sems.at[3]))
    if count == 4:
        copies[3].start()
    else:
        _, _, z, _ = here()
        inner = jnp.logical_or(z == 1, z == 2)
        pl.when(inner)(copies[3].start)
        pl.when(jnp.logical_not(inner))(pltpu.make_async_copy(pieces[4], buf.at[3], sems.at[3]).start)
    for d, copy in enumerate(copies):
        copy.wait()
        pltpu.make_async_copy(buf.at[d], out.at[d], sems.at[4 + d]).start()
    for d in range(4):
        pltpu.make_async_copy(buf.at[d], out.at[d], sems.at[4 + d]).wait()


def bundle(*pieces):
    shape = (4, *pieces[0].shape)
    return pl.pallas_call(
        functools.partial(bundle_kernel, len(pieces)),
        in_specs=[ANY] * len(pieces),
        out_specs=ANY,
        out_shape=jax.ShapeDtypeStruct(shape, pieces[0].dtype),
        scratch_shapes=[pltpu.VMEM(shape, pieces[0].dtype), pltpu.SemaphoreType.DMA((8,))],
        compiler_params=params(),
        cost_estimate=cost(1),
        name="bundle",
    )(*pieces)


def out_kernel(chunks, top, gate_own, gate_par, *refs):
    mine, theirs, refs = refs[: chunks - 1], refs[chunks - 1 : 2 * chunks - 2], refs[2 * chunks - 2 :]
    last_mine, last_theirs, pieces = refs[:4], refs[4:8], refs[8:12]
    terms, total, att, w, asems, wsems = refs[12:]
    devices, _, rows, _ = att.shape
    group, _, plane, core = here()
    span = slice(top, top + rows)
    waits = []
    for d in range(devices):
        pairs = []
        for j in range(chunks):
            got, given = (mine[j].at[d], theirs[j].at[d]) if j < chunks - 1 else (last_mine[d], last_theirs[d])
            at = pl.multiple_of(core * (chunks * HD) + j * HD, HD)
            pairs.append((got.at[:, span, :], att.at[d, :, :, pl.ds(at, HD)]))
            at = pl.multiple_of((1 - core) * (chunks * HD) + j * HD, HD)
            for i in range(2):
                pairs.append((given.at[1 - i, span, :], att.at[d, i, :, pl.ds(at, HD)]))
        waits.append([pltpu.make_async_copy(a, b, asems.at[3 * chunks * d + n]) for n, (a, b) in enumerate(pairs)])
    wcopies = []
    for d in range(devices):
        block = plane ^ d
        slot = (block // 2) ^ core
        swap = (block % 2) ^ group
        which = 2 * slot + swap
        for n, piece in enumerate(pieces):
            copy = pltpu.make_async_copy(piece, w.at[d], wsems.at[d])
            pl.when(which == n)(copy.start)
        wcopies.append(pltpu.make_async_copy(pieces[0], w.at[d], wsems.at[d]))
        for copy in waits[d]:
            copy.start()
    for d in range(devices):
        wcopies[d].wait()
        for copy in waits[d]:
            copy.wait()
        for i, gate in enumerate((gate_own, gate_par)):
            place = core if i == 0 else 1 - core
            part = (
                jnp.dot(att[d, i], w[d], preferred_element_type=jnp.float32).astype(jnp.bfloat16).astype(jnp.float32)
            )
            if d > 0:
                part = terms[place] + part
            if d == devices - 1:
                part = gate[...] * part
            terms[place] = part
    total[...] = (terms[0] + terms[1]).astype(total.dtype)


def out_projection(top, count, gate_own, gate_par, mine, theirs, last_mine, last_theirs, pieces):
    chunks = len(mine) + 1
    devices = mine[0].shape[0]
    deep, share = pieces[0].shape
    return pl.pallas_call(
        functools.partial(out_kernel, chunks, top),
        in_specs=[VMEM, VMEM] + [FREE] * (2 * chunks + 10),
        out_specs=[VMEM, VMEM],
        out_shape=[
            jax.ShapeDtypeStruct((2, count, share), jnp.float32),
            jax.ShapeDtypeStruct((count, share), CARRY),
        ],
        scratch_shapes=[
            pltpu.VMEM((devices, 2, count, deep), jnp.bfloat16),
            pltpu.VMEM((devices, deep, share), jnp.bfloat16),
            pltpu.SemaphoreType.DMA((devices * 3 * chunks,)),
            pltpu.SemaphoreType.DMA((devices,)),
        ],
        compiler_params=params(),
        cost_estimate=cost(12),
        name="out_projection",
    )(gate_own, gate_par, *mine, *theirs, *last_mine, *last_theirs, *pieces)


def close_kernel(terms, carry, far, own, par, mine, send, squares):
    _, t, _, core = here()
    first = core == 0
    low = jnp.where(first, own[...], par[...]).astype(jnp.float32)
    high = jnp.where(first, par[...], own[...]).astype(jnp.float32)
    at_low = jnp.where(t < 2, low, far[...].astype(jnp.float32)) + carry[...].astype(jnp.float32)
    at_high = at_low + terms[0]
    end = at_high + terms[1]
    mine[...] = jnp.where(first, at_high, end)
    send[...] = jnp.where(first, end, at_high)
    for n, gap in enumerate((at_low - low, at_high - high)):
        part = jnp.sum(gap * gap, axis=0, keepdims=True)

        @pl.when(pl.program_id(0) == 0)
        def _(n=n, part=part):
            squares[n : n + 1, :] = part

        @pl.when(pl.program_id(0) > 0)
        def _(n=n, part=part):
            squares[n : n + 1, :] += part


def close(top, terms, carry, far, own, par):
    _, count, share = terms.shape
    block = 192 if count % 192 == 0 and top % 192 == 0 else count
    skip = top // block
    whole = pl.BlockSpec((block, share), lambda i: (skip + i, 0))
    part = pl.BlockSpec((block, share), lambda i: (i, 0))
    return pl.pallas_call(
        close_kernel,
        grid=(count // block,),
        in_specs=[pl.BlockSpec((2, block, share), lambda i: (0, i, 0)), part, whole, whole, whole],
        out_specs=[part, part, pl.BlockSpec((2, share), lambda i: (0, 0))],
        out_shape=[
            jax.ShapeDtypeStruct((count, share), jnp.float32),
            jax.ShapeDtypeStruct((count, share), jnp.float32),
            jax.ShapeDtypeStruct((2, share), jnp.float32),
        ],
        compiler_params=params(),
        cost_estimate=cost(8),
        name="close",
    )(terms, carry, far, own, par)


def join_kernel(parts, *refs):
    mine, given, (out, buf, sems) = refs[:parts], refs[parts : 2 * parts], refs[2 * parts :]
    count, share = mine[0].shape
    _, _, _, core = here()
    copies = []
    for n, piece in enumerate((*mine, *given)):
        rows = slice((n % parts) * count, (n % parts + 1) * count)
        at = pl.multiple_of((core if n < parts else 1 - core) * share, HD)
        copies.append(
            (
                pltpu.make_async_copy(piece, buf.at[n], sems.at[2 * n]),
                pltpu.make_async_copy(buf.at[n], out.at[0, rows, pl.ds(at, share)], sems.at[2 * n + 1]),
            )
        )
    for come, _ in copies:
        come.start()
    for come, go in copies:
        come.wait()
        go.start()
    for _, go in copies:
        go.wait()


def join(mine, given):
    parts = len(mine)
    count, share = mine[0].shape
    return pl.pallas_call(
        functools.partial(join_kernel, parts),
        in_specs=[FREE] * (2 * parts),
        out_specs=ANY,
        out_shape=jax.ShapeDtypeStruct((1, parts * count, 2 * share), jnp.float32),
        scratch_shapes=[
            pltpu.VMEM((2 * parts, count, share), jnp.float32),
            pltpu.SemaphoreType.DMA((4 * parts,)),
        ],
        compiler_params=params(),
        cost_estimate=cost(8),
        name="join",
    )(*mine, *given)


def fast_body(
    states, timesteps, step_sizes, mod_scale, mod_gate, w_query, w_key, w_value, query_gain, key_gain, w_out
):
    latent = states[0]
    rows, width = latent.shape
    stamp = timesteps[0].astype(jnp.float32)
    t, z = lax.axis_index("tm"), lax.axis_index("tensor")
    core, chip = t % 2, t // 2
    devices = 4
    steps = range(4)
    share = mod_gate.shape[0] // 2
    chunks = w_query.shape[1] // (2 * HD)

    def over(array, axis, flip):
        return lax.ppermute(array, axis, [(i, i ^ flip) for i in range(lax.axis_size(axis))])

    def far(array):
        return over(array, "tm", 2)

    def swap(array):
        return over(array, "group", 1)

    def partner(array):
        return over(array, "tm", 1)

    def along(array, flip):
        return over(array, "tensor", flip)

    def middle(array):
        return lax.ppermute(array, "tensor", [(1, 2), (2, 1)])

    def outward(array):
        return lax.ppermute(array, "tensor", [(1, 0), (2, 3)])

    def place(group, step, tensor):
        return (group * 4 + step) * devices + tensor

    def cross(array):
        pairs = [(a * devices + b, (a ^ 2) * devices + b) for a in steps for b in range(devices) if a // 2 == b // 2]
        return lax.ppermute(array, ("tm", "tensor"), pairs)

    def to_plane(k, piece):
        pairs = [
            (place(b % 2, a, b), place(b % 2, 2 * (a // 2) + (k ^ (b // 2)), a))
            for a in steps
            for b in range(devices)
        ]
        return lax.ppermute(piece, ("group", "tm", "tensor"), pairs)

    weights = (w_query, w_key, w_value)
    others = [partner(w) for w in weights]
    own_step = jnp.stack([stamp, step_sizes[0]])
    par_step = partner(own_step)
    p0, r0 = first_packs(weights)
    p0, r0, w_out, states = phase(p0, r0, w_out, states)

    y0 = far(p0)
    z0 = over(r0, "tm", 3)
    base = z * (2 * share)
    lat_own = lax.dynamic_slice_in_dim(states[0], base + core * share, share, 1)
    lat_give = lax.dynamic_slice_in_dim(states[0], base + (1 - core) * share, share, 1)
    lat_par = partner(lat_give)
    hidden = fast_hidden(states, make_scale(stamp, mod_scale))
    s1, s2, o0, o1 = packs(weights, others, w_out)
    y0, z0, hidden, s1, s2, o0, o1, lat_own, lat_par, own_step, par_step = phase(
        y0, z0, hidden, s1, s2, o0, o1, lat_own, lat_par, own_step, par_step
    )

    beside = partner(hidden)
    y1, x0, xz0, sent0, sent1 = far(s1), swap(y0), swap(z0), to_plane(0, o0), to_plane(1, o1)
    acc = near(hidden, beside, (*weights, *others))
    y1, x0, xz0, acc, beside, s2, sent0 = phase(y1, x0, xz0, acc, beside, s2, sent0)

    x1, y2 = swap(y1), far(s2)
    att0 = attend(0, hidden, beside, acc, 0, (y0, z0, x0, xz0), query_gain, key_gain)
    att0, own_step, par_step, sent1 = phase(att0, own_step, par_step, sent1)
    two0, one0 = along(att0, 2), along(att0, 1)
    gates = []
    for pair in (own_step, par_step):
        gate = pair[1] * make_gate(pair[0], mod_gate, width)
        gates.append(lax.dynamic_slice_in_dim(gate, core * share, share, 0).reshape(1, share))
    y2, x1, acc, *gates = phase(y2, x1, acc, *gates)

    x2, u0, inner0 = swap(y2), cross(sent0), middle(att0)
    att1 = attend(1, hidden, beside, acc, 1, (y1, x1), query_gain, key_gain)
    att1, two0, v0 = phase(att1, two0, sent0)
    outer0, two1 = outward(two0), along(att1, 2)
    u0, x2, one0, inner0, outer0, v0 = phase(u0, x2, one0, inner0, outer0, v0)

    home = chip == z // 2
    v0 = jnp.where(home, v0, u0)
    xv0, u1 = swap(v0), cross(sent1)
    one1, inner1 = along(att1, 1), middle(att1)
    att2 = attend(2, hidden, beside, acc, 2, (y2, x2), query_gain, key_gain)
    two1, att2 = phase(two1, att2)
    outer1, two2 = outward(two1), along(att2, 2)
    g0 = bundle(att0, one0, two0, inner0, outer0)
    u1, xv0, v0, one1, inner1, outer1, g0, lat_own, lat_par, *gates = phase(
        u1, xv0, v0, one1, inner1, outer1, g0, lat_own, lat_par, *gates
    )
    gate_own, gate_par = gates

    one2 = along(att2, 1)
    v1 = jnp.where(home, sent1, u1)
    xv1 = swap(v1)
    start_far = lax.ppermute(jnp.where(core == 0, lat_own, lat_par), "tm", [(0, 2), (1, 3)])
    g1 = bundle(att1, one1, two1, inner1, outer1)
    two2, one2, v1, xv1, g1, start_far = phase(two2, one2, v1, xv1, g1, start_far)
    outer2, inner2 = outward(two2), middle(att2)
    q0, q1, b0, b1, b2 = partner(g0), partner(g1), partner(att2), partner(one2), partner(two2)
    outer2, inner2, q0, q1, b0, b1, b2 = phase(outer2, inner2, q0, q1, b0, b1, b2)

    three2 = jnp.where(jnp.logical_or(z == 1, z == 2), inner2, outer2)
    b3 = partner(three2)
    pieces = [v0, xv0, v1, xv1]

    count = rows // 2

    def project(top, gate_own):
        mine, theirs = [att2, one2, two2, three2], [b0, b1, b2, b3]
        return out_projection(top, count, gate_own, gate_par, [g0, g1], [q0, q1], mine, theirs, pieces)

    def ahead(total):
        return lax.ppermute(total, "tm", [(0, 2), (1, 3)])

    terms0, total0 = project(0, gate_own)
    terms0, total0, gate_own = phase(terms0, total0, gate_own)
    carry0 = ahead(total0)
    terms1, total1 = project(count, gate_own)
    terms1, total1, terms0 = phase(terms1, total1, terms0)
    carry1 = ahead(total1)
    own0, send0, squares0 = close(0, terms0, carry0, start_far, lat_own, lat_par)
    carry1, own0, send0, squares0 = phase(carry1, own0, send0, squares0)
    given0 = partner(send0)
    own1, send1, squares1 = close(count, terms1, carry1, start_far, lat_own, lat_par)
    given0, own1, send1, squares = phase(given0, own1, send1, squares0 + squares1)
    given1, squares_par = partner(send1), partner(squares)
    given1, squares = phase(given1, squares + squares_par)
    sums = jnp.sum(squares, axis=1)
    sums = sums + along(sums, 1) + along(sums, 2) + along(sums, 3)
    next_share = join([own0, own1], [given0, given1])
    errors = (lax.dynamic_slice_in_dim(sums, core, 1, 0) / (rows * width)).reshape(1, 1)
    return (next_share, errors)


def solution(mesh):
    placed = (
        P("tm", "group", None),
        P("tm"),
        P("tm"),
        P(),
        P("tensor"),
        P("tm", "tensor"),
        P("tm", "tensor"),
        P("tm", "tensor"),
        P("tensor"),
        P("tensor"),
        P("tensor", "tm"),
    )
    fast = mesh.shape["group"] == 2 and mesh.shape["tm"] == 4 and mesh.shape["tensor"] == 4
    return jax.shard_map(
        fast_body if fast else general_body,
        mesh=mesh,
        in_specs=placed,
        out_specs=(P("tm", "group", "tensor"), P("group", "tm")),
        check_vma=False,
    )
```
